512 devices in a mesh: ctx: 64 (over x, y, core), split: 8 (over z).
Axes of the slice: x: 4, y: 8, z: 8, core: 2. Of those that a mesh axis runs over, the one named last changes fastest.
Arguments:
- cache_keys: bfloat16 [64, 1024, 64, 128], P(None, ('ctx', 'split')), may hold values from -5 to 5
- cache_values: bfloat16 [64, 1024, 64, 128], P(None, ('ctx', 'split')), may hold values from -6 to 6
- counts: int32 [16, 1024], replicated, may hold values from 1 to 64, as said below
- listed: int32 [64, 256], replicated, may hold values from 0 to 1023, as said below
- queries: bfloat16 [64, 128, 16, 128], P('ctx'), may hold values from -100 to 100
Outputs:
- attended: float32 [64, 128, 16, 128], P('ctx')
The draws below stay inside these ranges and needn't reach their ends.
Inputs may be any that keep to these rules, and one draw needn't show every extreme that they name: listed[i] holds 256 distinct pages; of the 2 pages of one device (pages d * 2 to d * 2 + 1 of device d in ctx-major order) at most one is listed for an item; for every item all devices of one split index hold a listed page. Slots 0 to counts - 1 of a page are valid; the first listed page of every item is full.
All inputs are finite; a program needn't handle non-finite values.
Results may differ from the reference program's by a relative error of at most 0.005.
Values may be sent and summed in bfloat16 or wider, within the bound.
No kernel may reach another device: no remote copies, remote signals or barrier semaphores. Data moves between devices by JAX's collectives and lax.ppermute only.
A program may use at most 64 MiB of HBM per device.

```python
import jax
import jax.numpy as jnp
from jax import lax

HD = 128
KVH = 4
GQ = 16
PAGE = 64
PL = 2
QROWS = 128
R = 16
ITEMS = 64
NP = 1024
SEL = 256
N_CTX = 64
N_SPLIT = 8


def shared_lists(key):
    key = jax.random.fold_in(key, 7)
    total = N_CTX * N_SPLIT

    def one_item(item_key):
        first, second, third = jax.random.split(item_key, 3)
        full_split = jax.random.randint(first, (), 0, N_SPLIT)
        order_keys = jax.random.permutation(second, total).astype(jnp.int32)
        source = jnp.arange(total, dtype=jnp.int32)
        score = jnp.where(source % N_SPLIT == full_split, order_keys - total, order_keys)
        chosen = jnp.argsort(score, stable=True)[:SEL].astype(jnp.int32)
        which = jax.random.randint(third, (SEL,), 0, PL)
        return (chosen * PL + which).astype(jnp.int32)
    lists = jax.vmap(one_item)(jax.random.split(key, ITEMS))
    return lists


def draw_listed(key, part):
    lists = shared_lists(key)
    return lists


def draw_counts(key, part):
    lists = shared_lists(key)
    key = jax.random.fold_in(key, 3)
    filled = jax.random.randint(key, (R, NP), 1, PAGE + 1)
    request = jnp.arange(ITEMS, dtype=jnp.int32) // KVH
    filled = filled.at[request, lists[:, 0]].set(PAGE)
    return filled.astype(jnp.int32)


def draw_cache_keys(key, part):
    key = jax.random.fold_in(key, 5)
    entries = jnp.clip(jax.random.normal(key, (ITEMS, NP, PAGE, HD), jnp.float32), -5.0, 5.0)
    return entries.astype(jnp.bfloat16)


def draw_queries(key, part):
    key = jax.random.fold_in(key, 9)
    entries = jnp.clip(2.0 * jax.random.normal(key, (ITEMS, QROWS, GQ, HD), jnp.float32), -12.0, 12.0)
    return entries.astype(jnp.bfloat16)


def shard_levels(stream_key, dims, cuts, smallest, top_value):
    factor_of, own = 1.0, jax.random.fold_in(stream_key, 6)
    for position, parts in cuts:
        heights = jnp.exp(jax.random.uniform(jax.random.fold_in(own, position), (parts,), jnp.float32, smallest / len(cuts), top_value / len(cuts)))
        factor_of = factor_of * jnp.repeat(heights, dims[position] // parts).reshape([-1 if axis == position else 1 for axis in range(len(dims))])
    return factor_of


def normal_values(stream_key, extent, scale, limit, cuts=(), kind=jnp.bfloat16):
    gain = shard_levels(stream_key, extent, cuts, -0.22, 0.18) if cuts else 1.0
    array = jax.random.normal(stream_key, extent, jnp.float32) * scale * gain
    return jnp.minimum(jnp.maximum(array, -limit), limit).astype(kind)


def setup_inputs(seed: int = 0) -> dict:
    arg_keys = jax.random.split(jax.random.key(seed), 6)
    return {
        "cache_keys": draw_cache_keys(jax.random.fold_in(arg_keys[5], 71), 0),
        "cache_values": normal_values(arg_keys[1], (ITEMS, NP, PAGE, HD), 1.0, 6.0, ((1, 512),)),
        "counts": draw_counts(jax.random.fold_in(arg_keys[5], 71), 0),
        "listed": draw_listed(jax.random.fold_in(arg_keys[5], 71), 0),
        "queries": draw_queries(jax.random.fold_in(arg_keys[5], 71), 0),
    }


NEG = -1.0e30


def reference(cache_keys, cache_values, counts, listed, queries):
    scale = HD ** -0.5
    tok = jnp.arange(PAGE, dtype=jnp.int32)
    request = (jnp.arange(ITEMS, dtype=jnp.int32) // KVH).astype(jnp.int32)
    item_counts = counts[request]

    def per_item(args):
        keys_i, vals_i, cnt_row, sel_i, q_i = args
        valid = (tok[None, :] < cnt_row[:, None]).astype(jnp.float32)
        cnt_f = cnt_row.astype(jnp.float32)
        mean_keys = (jnp.einsum('pt,ptd->pd', valid, keys_i.astype(jnp.float32)) / cnt_f[:, None]).astype(jnp.bfloat16)
        mean_values = (jnp.einsum('pt,ptd->pd', valid, vals_i.astype(jnp.float32)) / cnt_f[:, None]).astype(jnp.bfloat16)
        rows = q_i.reshape(-1, HD)
        marked = jnp.zeros((NP,), jnp.float32).at[sel_i].set(1.0) > 0.5
        cscore = jnp.dot(rows, mean_keys.T, preferred_element_type=jnp.float32) * scale + jnp.log(cnt_f)[None, :]
        cscore = jnp.where(marked[None, :], NEG, cscore)
        klist = keys_i[sel_i].reshape(-1, HD)
        vlist = vals_i[sel_i].reshape(-1, HD)
        live = (tok[None, :] < cnt_row[sel_i][:, None]).reshape(-1)
        escore = jnp.dot(rows, klist.T, preferred_element_type=jnp.float32) * scale
        escore = jnp.where(live[None, :], escore, NEG)
        top = jnp.maximum(jnp.max(cscore, axis=1), jnp.max(escore, axis=1))
        cweight = jnp.where(marked[None, :], 0.0, jnp.exp(cscore - top[:, None]))
        eweight = jnp.where(live[None, :], jnp.exp(escore - top[:, None]), 0.0)
        total = jnp.sum(cweight, axis=1) + jnp.sum(eweight, axis=1)
        numer = jnp.dot(eweight.astype(jnp.bfloat16), vlist, preferred_element_type=jnp.float32)
        numer = numer + jnp.dot(cweight.astype(jnp.bfloat16), mean_values, preferred_element_type=jnp.float32)
        return (numer / total[:, None]).reshape(q_i.shape)

    return lax.map(per_item, (cache_keys, cache_values, item_counts, listed, queries))
```

```python
import functools

import jax
import jax.numpy as jnp
from jax import lax
from jax.experimental import pallas as pl
from jax.experimental.pallas import tpu as pltpu
from jax.sharding import PartitionSpec as P

NEG = -1e30
LOG2E = 1.4426950408889634

PAGE = 64
HEAD = 128
TAIL = 8
ROWS = 2 * PAGE + TAIL
MiB = 1024 * 1024


def pack_kernel(page_ref, count_ref, listed_ref, keys_ref, values_ref, out_ref, cache, message, got, sent):
    items = out_ref.shape[0]
    kv_heads = 4
    block = 8
    groups = items // block

    def fetch(g):
        at = pl.ds(g * block, block)
        return [
            pltpu.make_async_copy(ref.at[at], cache.at[at, a], got.at[a, g])
            for a, ref in enumerate((keys_ref, values_ref))
        ]

    def send(g):
        at = pl.ds(g * block, block)
        return pltpu.make_async_copy(message.at[at], out_ref.at[at], sent.at[g])

    for g in range(groups):
        for copy in fetch(g):
            copy.start()
    second = jnp.max(
        jnp.where(listed_ref[...] == page_ref[0] + 1, 1.0, 0.0), axis=1, keepdims=True
    )
    row = lax.broadcasted_iota(jnp.int32, (16, 4 * PAGE), 0)
    slot = lax.broadcasted_iota(jnp.int32, (16, 4 * PAGE), 1)
    quarter = slot // PAGE
    slot = slot % PAGE
    out_row = lax.broadcasted_iota(jnp.int32, (16, HEAD), 0)
    for g in range(groups):
        for copy in fetch(g):
            copy.wait()
        for item in range(g * block, (g + 1) * block):
            if item % kv_heads == 0:
                request = item // kv_heads
                count = [count_ref[2 * request], count_ref[2 * request + 1]]
                limit = jnp.where(row % 2 == 0, count[0], count[1])
                live = jnp.logical_and(quarter == row, slot < limit)
                live = jnp.where(live, 1.0, 0.0).astype(jnp.bfloat16)
                divisor = jnp.where(out_row % 2 == 0, count[0], count[1]).astype(jnp.float32)
                inverse = 1.0 / divisor
            choice = jnp.broadcast_to(second[item : item + 1, :], (PAGE, HEAD)) > 0.5
            for a in range(2):
                message[item, a * PAGE : (a + 1) * PAGE, :] = jnp.where(
                    choice, cache[item, a, 1], cache[item, a, 0]
                )
            both = cache[item].reshape(4 * PAGE, HEAD)
            total = jnp.dot(live, both, preferred_element_type=jnp.float32)
            message[item, 2 * PAGE : ROWS, :] = (total * inverse)[:TAIL].astype(jnp.bfloat16)
        send(g).start()
    for g in range(groups):
        send(g).wait()


def pack(page, local_counts, listed, cache_keys, cache_values):
    items = cache_keys.shape[0]
    groups = items // 8
    whole = pl.BlockSpec(memory_space=pl.ANY)
    scalars = pl.BlockSpec(memory_space=pltpu.SMEM)
    return pl.pallas_call(
        pack_kernel,
        in_specs=[scalars, scalars, pl.BlockSpec(memory_space=pltpu.VMEM), whole, whole],
        out_specs=whole,
        out_shape=jax.ShapeDtypeStruct((items, ROWS, HEAD), jnp.bfloat16),
        scratch_shapes=[
            pltpu.VMEM((items, 2, 2, PAGE, HEAD), jnp.bfloat16),
            pltpu.VMEM((items, ROWS, HEAD), jnp.bfloat16),
            pltpu.SemaphoreType.DMA((2, groups)),
            pltpu.SemaphoreType.DMA((groups,)),
        ],
        compiler_params=pltpu.CompilerParams(vmem_limit_bytes=58 * MiB),
        name="pack",
    )(page, local_counts, listed, cache_keys, cache_values)


def split3(x):
    high = x.astype(jnp.bfloat16).astype(jnp.float32)
    rest = x - high
    middle = rest.astype(jnp.bfloat16).astype(jnp.float32)
    return high, middle, rest - middle


def attend_kernel(
    live_ref, cbias_ref, got_ref, q_ref, out_ref, ka, vv, vt, qt, sc0, sc1, acc, *, chunk, c2
):
    sources = got_ref.shape[0]
    cents = 2 * sources
    block = qt.shape[2]
    width = out_ref.shape[2]
    blocks = q_ref.shape[0] // block
    sc = (sc0, sc1)
    lane = lax.broadcasted_iota(jnp.int32, (PAGE, HEAD), 1)
    tok = lax.broadcasted_iota(jnp.int32, (PAGE, HEAD), 0)
    vt[HEAD:, :] = jnp.ones((vt.shape[0] - HEAD, vt.shape[1]), jnp.bfloat16)
    for i in range(2):
        qt[i, HEAD:, :] = jnp.ones((HEAD, block), jnp.bfloat16)

    tails = got_ref[:, 2 * PAGE : ROWS, :].astype(jnp.float32).reshape(sources * TAIL, HEAD)
    tails = tails.astype(jnp.bfloat16)
    r = lax.broadcasted_iota(jnp.int32, (cents, sources * TAIL), 0)
    c = lax.broadcasted_iota(jnp.int32, (cents, sources * TAIL), 1)
    first = (r // 2) * TAIL + r % 2
    for off, ref in ((0, ka), (2, vv)):
        chosen = (c == first + off).astype(jnp.float32).astype(jnp.bfloat16)
        ref[0:cents, :HEAD] = jnp.dot(
            chosen, tails, preferred_element_type=jnp.float32
        ).astype(jnp.bfloat16)
    high, middle, low = split3(jnp.transpose(jnp.broadcast_to(cbias_ref[...], (cents, cents))))
    clane = lax.broadcasted_iota(jnp.int32, (cents, HEAD), 1)
    bias = jnp.where(clane == 0, high, jnp.where(clane == 1, middle, low))
    ka[0:cents, HEAD:] = jnp.where(clane < 3, bias, 0.0).astype(jnp.bfloat16)

    def place(s, at):
        rows = pl.ds(pl.multiple_of(at, 16), PAGE)
        live = live_ref[s]
        ka[rows, :HEAD] = got_ref[s, 0:PAGE, :]
        vv[rows, :] = got_ref[s, PAGE : 2 * PAGE, :]
        dead = jnp.logical_and(lane == 0, tok >= live)
        ka[rows, HEAD:] = jnp.where(dead, NEG, 0.0).astype(jnp.bfloat16)
        return at + ((live + 15) // 16) * 16

    end = lax.fori_loop(0, sources, place, cents)
    dead = jnp.where(lane == 0, NEG, 0.0).astype(jnp.bfloat16)
    for k in range(0, chunk, PAGE):
        rows = pl.ds(pl.multiple_of(end + k, 16), PAGE)
        ka[rows, :HEAD] = jnp.zeros((PAGE, HEAD), jnp.bfloat16)
        ka[rows, HEAD:] = dead
        vv[rows, :] = jnp.zeros((PAGE, HEAD), jnp.bfloat16)
    chunks = (end + chunk - 1) // chunk

    def turn(j, carry):
        for k in range(0, chunk, HEAD):
            at = pl.ds(pl.multiple_of(j * chunk + k, HEAD), HEAD)
            vt[:HEAD, at] = jnp.transpose(vv[at, :].astype(jnp.float32)).astype(jnp.bfloat16)
        return carry

    lax.fori_loop(0, chunks, turn, 0)

    top = None
    for b in range(blocks + 1):
        if b < blocks:
            rows = q_ref[b * block : (b + 1) * block, :].astype(jnp.float32)
            qt[b % 2, :HEAD, :] = jnp.transpose(rows).astype(jnp.bfloat16)
        if b > 0:
            acc[...] = jnp.zeros_like(acc)

        def body(j, best, b=b, top=top):
            at = pl.ds(pl.multiple_of(j * chunk, chunk), chunk)
            if b > 0:
                weight = jnp.exp2((sc[(b - 1) % 2][at, :] - top) * c2).astype(jnp.bfloat16)
                acc[...] += jnp.dot(vt[:, at], weight, preferred_element_type=jnp.float32)
            if b < blocks:
                score = jnp.dot(ka[at, :], qt[b % 2], preferred_element_type=jnp.float32)
                sc[b % 2][at, :] = score
                best = jnp.maximum(best, jnp.max(score.reshape(chunk // 8, 8, block), axis=0))
            return best

        best = lax.fori_loop(0, chunks, body, jnp.full((8, block), 4 * NEG, jnp.float32))
        if b > 0:
            total = acc[HEAD : HEAD + 1, :]
            out = (acc[:HEAD, :] / total).astype(jnp.bfloat16)
            row = lax.broadcasted_iota(jnp.int32, (TAIL, block), 0)
            tile = jnp.zeros((TAIL, block), jnp.float32)
            for i, piece in enumerate(split3(top) + split3(total)):
                tile = jnp.where(row == i, piece, tile)
            tile = tile.astype(jnp.bfloat16)
            for k in range(block // width):
                to = (b - 1) * (block // width) + k
                out_ref[to, :HEAD, :] = out[:, k * width : (k + 1) * width]
                out_ref[to, HEAD:, :] = tile[:, k * width : (k + 1) * width]
        top = jnp.max(best, axis=0, keepdims=True)


def attend(live, cbias, got, rows, parts, c2):
    sources = got.shape[0]
    chunk = 512
    block = 512
    keys = sources * (PAGE + 2)
    padded = pl.cdiv(keys, chunk) * chunk
    width = rows.shape[0] // parts
    vmem = pl.BlockSpec(memory_space=pltpu.VMEM)
    return pl.pallas_call(
        functools.partial(attend_kernel, chunk=chunk, c2=c2),
        in_specs=[pl.BlockSpec(memory_space=pltpu.SMEM), vmem, vmem, vmem],
        out_specs=vmem,
        scratch_shapes=[
            pltpu.VMEM((padded + chunk, 2 * HEAD), jnp.bfloat16),
            pltpu.VMEM((padded + chunk, HEAD), jnp.bfloat16),
            pltpu.VMEM((HEAD + 16, padded), jnp.bfloat16),
            pltpu.VMEM((2, 2 * HEAD, block), jnp.bfloat16),
            pltpu.VMEM((padded, block), jnp.float32),
            pltpu.VMEM((padded, block), jnp.float32),
            pltpu.VMEM((HEAD + 16, block), jnp.float32),
        ],
        out_shape=jax.ShapeDtypeStruct((parts, HEAD + TAIL, width), jnp.bfloat16),
        compiler_params=pltpu.CompilerParams(vmem_limit_bytes=36 * MiB),
        cost_estimate=pl.CostEstimate(
            flops=4 * rows.shape[0] * keys * HEAD,
            bytes_accessed=4 * MiB,
            transcendentals=rows.shape[0] * keys,
        ),
        name="attend",
    )(live, cbias, got, rows)


def merge_kernel(got_ref, out_ref, *, c2):
    parts = got_ref.shape[0]
    tops, totals = [], []
    for z in range(parts):
        tile = got_ref[z, HEAD:, :].astype(jnp.float32)
        tops.append(tile[0:1] + tile[1:2] + tile[2:3])
        totals.append(tile[3:4] + tile[4:5] + tile[5:6])
    top = functools.reduce(jnp.maximum, tops)
    factors = [t * jnp.exp2((m - top) * c2) for m, t in zip(tops, totals)]
    whole = functools.reduce(jnp.add, factors)
    out = jnp.zeros(got_ref.shape[1:], jnp.float32)[:HEAD]
    for z in range(parts):
        out += got_ref[z, :HEAD, :].astype(jnp.float32) * (factors[z] / whole)
    out = jnp.transpose(out).astype(jnp.bfloat16)
    for z in range(parts):
        out_ref[z] = out


def merge(got, c2):
    parts, unused, block = got.shape
    return pl.pallas_call(
        functools.partial(merge_kernel, c2=c2),
        out_shape=jax.ShapeDtypeStruct((parts, block, HEAD), jnp.bfloat16),
        compiler_params=pltpu.CompilerParams(vmem_limit_bytes=16 * MiB),
        name="merge",
    )(got)


def local(cache_keys, cache_values, counts, listed, queries):
    ctx_n = lax.axis_size("ctx")
    split_n = lax.axis_size("split")
    items, pages_here, page_len, head = cache_keys.shape
    requests = counts.shape[0]
    kv_heads = items // requests
    root = head**0.5
    c2 = head**-0.5 * LOG2E
    item = lax.axis_index("ctx")
    split_idx = lax.axis_index("split")
    first = (item * split_n + split_idx) * pages_here
    local_counts = lax.dynamic_slice_in_dim(counts, first, pages_here, 1).reshape(-1)
    message = pack(first.reshape(1), local_counts, listed, cache_keys, cache_values)
    got = lax.all_to_all(message, "ctx", split_axis=0, concat_axis=0, tiled=True)

    sel_row = lax.dynamic_index_in_dim(listed, item, 0, keepdims=False)
    count_row = lax.dynamic_index_in_dim(counts, item // kv_heads, 0, keepdims=False)
    mine = count_row.reshape(ctx_n, split_n, pages_here)
    mine = lax.dynamic_index_in_dim(mine, split_idx, 1, keepdims=False)
    source = jnp.arange(ctx_n, dtype=jnp.int32)[:, None]
    candidate = (source * split_n + split_idx) * pages_here + jnp.arange(
        pages_here, dtype=jnp.int32
    )
    marks = jnp.any(sel_row[None, None, :] == candidate[:, :, None], axis=2)
    live = jnp.sum(jnp.where(marks, mine, 0), axis=1)
    cbias = jnp.where(marks, NEG, jnp.log(mine.astype(jnp.float32)) * root)
    rows = queries.reshape(-1, head)
    partial = attend(live, cbias.reshape(1, -1), got, rows, split_n, c2)
    shared = lax.all_to_all(partial, "split", split_axis=0, concat_axis=0, tiled=True)
    out = lax.all_to_all(merge(shared, c2), "split", split_axis=0, concat_axis=0, tiled=True)
    return out.astype(jnp.float32).reshape(queries.shape)


def solution(mesh):
    return jax.shard_map(
        local,
        mesh=mesh,
        in_specs=(
            P(None, ("ctx", "split"), None, None),
            P(None, ("ctx", "split"), None, None),
            P(),
            P(),
            P("ctx", None, None, None),
        ),
        out_specs=P("ctx", None, None, None),
        check_vma=False,
    )
```

```python
import functools

import jax
import jax.numpy as jnp
from jax import lax
from jax.experimental import pallas as pl
from jax.experimental.pallas import tpu as pltpu
from jax.sharding import PartitionSpec as P

NEG = -1e30
LOG2E = 1.4426950408889634

PAGE = 64
HEAD = 128
TAIL = 8
ROWS = 2 * PAGE + TAIL
MiB = 1024 * 1024


def pack_kernel(
    page_ref,
    counts_ref,
    listed_ref,
    keys_ref,
    values_ref,
    out_ref,
    cache,
    message,
    count_here,
    listed,
    got,
    sent,
    small,
):
    items = out_ref.shape[0]
    page = page_ref[0]
    kv_heads = 4
    block = 8
    groups = items // block

    def fetch(g):
        at = pl.ds(g * block, block)
        return [
            pltpu.make_async_copy(ref.at[at], cache.at[at, a], got.at[a, g])
            for a, ref in enumerate((keys_ref, values_ref))
        ]

    def send(g):
        at = pl.ds(g * block, block)
        return pltpu.make_async_copy(message.at[at], out_ref.at[at], sent.at[g])

    columns = pl.ds(pl.multiple_of((page // HEAD) * HEAD, HEAD), HEAD)
    lists = pltpu.make_async_copy(listed_ref, listed, small.at[0])
    numbers = pltpu.make_async_copy(counts_ref.at[:, columns], count_here, small.at[1])
    lists.start()
    numbers.start()
    for g in range(groups):
        for copy in fetch(g):
            copy.start()
    lists.wait()
    second = jnp.max(jnp.where(listed[...] == page + 1, 1.0, 0.0), axis=1, keepdims=True)
    numbers.wait()
    row = lax.broadcasted_iota(jnp.int32, (16, 4 * PAGE), 0)
    slot = lax.broadcasted_iota(jnp.int32, (16, 4 * PAGE), 1)
    quarter = slot // PAGE
    slot = slot % PAGE
    out_row = lax.broadcasted_iota(jnp.int32, (16, HEAD), 0)
    for g in range(groups):
        for copy in fetch(g):
            copy.wait()
        for item in range(g * block, (g + 1) * block):
            if item % kv_heads == 0:
                request = item // kv_heads
                count = [count_here[request, page % HEAD + p] for p in range(2)]
                limit = jnp.where(row % 2 == 0, count[0], count[1])
                live = jnp.logical_and(quarter == row, slot < limit)
                live = jnp.where(live, 1.0, 0.0).astype(jnp.bfloat16)
                divisor = jnp.where(out_row % 2 == 0, count[0], count[1]).astype(jnp.float32)
                inverse = 1.0 / divisor
            choice = jnp.broadcast_to(second[item : item + 1, :], (PAGE, HEAD)) > 0.5
            for a in range(2):
                message[item, a * PAGE : (a + 1) * PAGE, :] = jnp.where(
                    choice, cache[item, a, 1], cache[item, a, 0]
                )
            both = cache[item].reshape(4 * PAGE, HEAD)
            total = jnp.dot(live, both, preferred_element_type=jnp.float32)
            message[item, 2 * PAGE : ROWS, :] = (total * inverse)[:TAIL].astype(jnp.bfloat16)
        send(g).start()
    for g in range(groups):
        send(g).wait()


def pack(page, counts, listed, cache_keys, cache_values):
    items = cache_keys.shape[0]
    groups = items // 8
    whole = pl.BlockSpec(memory_space=pl.ANY)
    return pl.pallas_call(
        pack_kernel,
        in_specs=[pl.BlockSpec(memory_space=pltpu.SMEM), whole, whole, whole, whole],
        out_specs=whole,
        out_shape=jax.ShapeDtypeStruct((items, ROWS, HEAD), jnp.bfloat16),
        scratch_shapes=[
            pltpu.VMEM((items, 2, 2, PAGE, HEAD), jnp.bfloat16),
            pltpu.VMEM((items, ROWS, HEAD), jnp.bfloat16),
            pltpu.SMEM((counts.shape[0], HEAD), jnp.int32),
            pltpu.VMEM(listed.shape, jnp.int32),
            pltpu.SemaphoreType.DMA((2, groups)),
            pltpu.SemaphoreType.DMA((groups,)),
            pltpu.SemaphoreType.DMA((2,)),
        ],
        compiler_params=pltpu.CompilerParams(vmem_limit_bytes=58 * MiB),
        name="pack",
    )(page, counts, listed, cache_keys, cache_values)


def split3(x):
    high = x.astype(jnp.bfloat16).astype(jnp.float32)
    rest = x - high
    middle = rest.astype(jnp.bfloat16).astype(jnp.float32)
    return high, middle, rest - middle


def attend_kernel(
    live_ref, cbias_ref, got_ref, q_ref, out_ref, ka, kt, vv, qa, sc0, sc1, best, top, acc, *, chunk, c2
):
    sources = got_ref.shape[0]
    cents = 2 * sources
    block = qa.shape[1]
    width = out_ref.shape[1] - 16
    blocks = q_ref.shape[0] // block
    sc = (sc0, sc1)
    lane = lax.broadcasted_iota(jnp.int32, (PAGE, HEAD), 1)
    tok = lax.broadcasted_iota(jnp.int32, (PAGE, HEAD), 0)
    vv[:, HEAD:] = jnp.ones((vv.shape[0], HEAD), jnp.bfloat16)
    for i in range(2):
        qa[i, :, HEAD:] = jnp.ones((block, HEAD), jnp.bfloat16)

    tails = got_ref[:, 2 * PAGE : ROWS, :].astype(jnp.float32).reshape(sources * TAIL, HEAD)
    tails = tails.astype(jnp.bfloat16)
    r = lax.broadcasted_iota(jnp.int32, (cents, sources * TAIL), 0)
    c = lax.broadcasted_iota(jnp.int32, (cents, sources * TAIL), 1)
    first = (r // 2) * TAIL + r % 2
    for off, ref in ((0, ka), (2, vv)):
        chosen = (c == first + off).astype(jnp.float32).astype(jnp.bfloat16)
        ref[0:cents, :HEAD] = jnp.dot(
            chosen, tails, preferred_element_type=jnp.float32
        ).astype(jnp.bfloat16)
    high, middle, low = split3(jnp.transpose(jnp.broadcast_to(cbias_ref[...], (cents, cents))))
    clane = lax.broadcasted_iota(jnp.int32, (cents, HEAD), 1)
    bias = jnp.where(clane == 0, high, jnp.where(clane == 1, middle, low))
    ka[0:cents, HEAD:] = jnp.where(clane < 3, bias, 0.0).astype(jnp.bfloat16)

    def place(s, at):
        rows = pl.ds(pl.multiple_of(at, 16), PAGE)
        live = live_ref[s]
        ka[rows, :HEAD] = got_ref[s, 0:PAGE, :]
        vv[rows, :HEAD] = got_ref[s, PAGE : 2 * PAGE, :]
        dead = jnp.logical_and(lane == 0, tok >= live)
        ka[rows, HEAD:] = jnp.where(dead, NEG, 0.0).astype(jnp.bfloat16)
        return at + ((live + 15) // 16) * 16

    end = lax.fori_loop(0, sources, place, cents)
    dead = jnp.where(lane == 0, NEG, 0.0).astype(jnp.bfloat16)
    for k in range(0, chunk, PAGE):
        rows = pl.ds(pl.multiple_of(end + k, 16), PAGE)
        ka[rows, :HEAD] = jnp.zeros((PAGE, HEAD), jnp.bfloat16)
        ka[rows, HEAD:] = dead
        vv[rows, :HEAD] = jnp.zeros((PAGE, HEAD), jnp.bfloat16)
    chunks = (end + chunk - 1) // chunk

    def turn(j, carry):
        for k in range(0, chunk, HEAD):
            at = pl.ds(pl.multiple_of(j * chunk + k, HEAD), HEAD)
            for half in (slice(0, HEAD), slice(HEAD, 2 * HEAD)):
                kt[half, at] = jnp.transpose(ka[at, half].astype(jnp.float32)).astype(jnp.bfloat16)
        return carry

    lax.fori_loop(0, chunks, turn, 0)

    lanes = lax.broadcasted_iota(jnp.int32, (block, HEAD), 1)
    for b in range(blocks + 1):
        if b < blocks:
            qa[b % 2, :, :HEAD] = q_ref[b * block : (b + 1) * block, :]
            best[...] = jnp.full((block, HEAD), 4 * NEG, jnp.float32)
        if b > 0:
            acc[...] = jnp.zeros_like(acc)

        def body(j, carry, b=b):
            at = pl.ds(pl.multiple_of(j * chunk, chunk), chunk)
            if b > 0:
                tops = jnp.concatenate([top[...]] * (chunk // HEAD), axis=1)
                weight = jnp.exp2((sc[(b - 1) % 2][:, at] - tops) * c2).astype(jnp.bfloat16)
                acc[...] += jnp.dot(weight, vv[at, :], preferred_element_type=jnp.float32)
            if b < blocks:
                score = jnp.dot(qa[b % 2], kt[:, at], preferred_element_type=jnp.float32)
                sc[b % 2][:, at] = score
                parts = [score[:, k : k + HEAD] for k in range(0, chunk, HEAD)]
                best[...] = functools.reduce(jnp.maximum, parts, best[...])
            return carry

        lax.fori_loop(0, chunks, body, 0)
        if b > 0:
            total = acc[:, HEAD:]
            out = (acc[:, :HEAD] / total).astype(jnp.bfloat16)
            stats = jnp.transpose(jnp.where(lanes == 0, top[...], total))
            pieces = split3(stats[0:1, :]) + split3(stats[1:2, :])
            row = lax.broadcasted_iota(jnp.int32, (16, HEAD), 0)
            for k in range(block // width):
                to = (b - 1) * (block // width) + k
                out_ref[to, :width, :] = out[k * width : (k + 1) * width, :]
                tile = jnp.zeros((16, HEAD), jnp.float32)
                for i, piece in enumerate(pieces):
                    for h in range(2):
                        from_ = k * width + h * HEAD
                        tile = jnp.where(row == 2 * i + h, piece[:, from_ : from_ + HEAD], tile)
                out_ref[to, width:, :] = tile.astype(jnp.bfloat16)
        if b < blocks:
            top[...] = jnp.broadcast_to(jnp.max(best[...], axis=1, keepdims=True), (block, HEAD))


def attend(live, cbias, got, rows, parts, c2):
    sources = got.shape[0]
    chunk = 512
    block = 512
    keys = sources * (PAGE + 2)
    padded = pl.cdiv(keys, chunk) * chunk
    width = rows.shape[0] // parts
    vmem = pl.BlockSpec(memory_space=pltpu.VMEM)
    return pl.pallas_call(
        functools.partial(attend_kernel, chunk=chunk, c2=c2),
        in_specs=[pl.BlockSpec(memory_space=pltpu.SMEM), vmem, vmem, vmem],
        out_specs=vmem,
        scratch_shapes=[
            pltpu.VMEM((padded + chunk, 2 * HEAD), jnp.bfloat16),
            pltpu.VMEM((2 * HEAD, padded), jnp.bfloat16),
            pltpu.VMEM((padded + chunk, 2 * HEAD), jnp.bfloat16),
            pltpu.VMEM((2, block, 2 * HEAD), jnp.bfloat16),
            pltpu.VMEM((block, padded), jnp.float32),
            pltpu.VMEM((block, padded), jnp.float32),
            pltpu.VMEM((block, HEAD), jnp.float32),
            pltpu.VMEM((block, HEAD), jnp.float32),
            pltpu.VMEM((block, 2 * HEAD), jnp.float32),
        ],
        out_shape=jax.ShapeDtypeStruct((parts, width + 16, HEAD), jnp.bfloat16),
        compiler_params=pltpu.CompilerParams(vmem_limit_bytes=40 * MiB),
        cost_estimate=pl.CostEstimate(
            flops=4 * rows.shape[0] * keys * HEAD,
            bytes_accessed=4 * MiB,
            transcendentals=rows.shape[0] * keys,
        ),
        name="attend",
    )(live, cbias, got, rows)


def merge_kernel(got_ref, out_ref, *, c2):
    parts = got_ref.shape[0]
    block = out_ref.shape[1]
    tops, totals = [], []
    for z in range(parts):
        tile = got_ref[z, block:, :].astype(jnp.float32)
        tops.append(tile[0:2] + tile[2:4] + tile[4:6])
        totals.append(tile[6:8] + tile[8:10] + tile[10:12])
    top = functools.reduce(jnp.maximum, tops)
    factors = [t * jnp.exp2((m - top) * c2) for m, t in zip(tops, totals)]
    whole = functools.reduce(jnp.add, factors)
    columns = jnp.transpose(jnp.concatenate([f / whole for f in factors], axis=0))
    for h in range(2):
        at = slice(h * HEAD, (h + 1) * HEAD)
        out = jnp.zeros((HEAD, HEAD), jnp.float32)
        for z in range(parts):
            column = columns[:, 2 * z + h : 2 * z + h + 1]
            out += got_ref[z, at, :].astype(jnp.float32) * column
        out = out.astype(jnp.bfloat16)
        for z in range(parts):
            out_ref[z, at, :] = out


def merge(got, c2):
    parts, block, unused = got.shape
    block -= 16
    return pl.pallas_call(
        functools.partial(merge_kernel, c2=c2),
        out_shape=jax.ShapeDtypeStruct((parts, block, HEAD), jnp.bfloat16),
        compiler_params=pltpu.CompilerParams(vmem_limit_bytes=16 * MiB),
        name="merge",
    )(got)


def local(cache_keys, cache_values, counts, listed, queries):
    ctx_n = lax.axis_size("ctx")
    split_n = lax.axis_size("split")
    items, pages_here, page_len, head = cache_keys.shape
    requests = counts.shape[0]
    kv_heads = items // requests
    root = head**0.5
    c2 = head**-0.5 * LOG2E
    item = lax.axis_index("ctx")
    split_idx = lax.axis_index("split")
    first = (item * split_n + split_idx) * pages_here
    message = pack(first.reshape(1), counts, listed, cache_keys, cache_values)
    got = lax.all_to_all(message, "ctx", split_axis=0, concat_axis=0, tiled=True)

    sel_row = lax.dynamic_index_in_dim(listed, item, 0, keepdims=False)
    count_row = lax.dynamic_index_in_dim(counts, item // kv_heads, 0, keepdims=False)
    mine = count_row.reshape(ctx_n, split_n, pages_here)
    mine = lax.dynamic_index_in_dim(mine, split_idx, 1, keepdims=False)
    source = jnp.arange(ctx_n, dtype=jnp.int32)[:, None]
    candidate = (source * split_n + split_idx) * pages_here + jnp.arange(
        pages_here, dtype=jnp.int32
    )
    marks = jnp.any(sel_row[None, None, :] == candidate[:, :, None], axis=2)
    live = jnp.sum(jnp.where(marks, mine, 0), axis=1)
    cbias = jnp.where(marks, NEG, jnp.log(mine.astype(jnp.float32)) * root)
    rows = queries.reshape(-1, head)
    partial = attend(live, cbias.reshape(1, -1), got, rows, split_n, c2)
    shared = lax.all_to_all(partial, "split", split_axis=0, concat_axis=0, tiled=True)
    out = lax.all_to_all(merge(shared, c2), "split", split_axis=0, concat_axis=0, tiled=True)
    return out.astype(jnp.float32).reshape(queries.shape)


def solution(mesh):
    return jax.shard_map(
        local,
        mesh=mesh,
        in_specs=(
            P(None, ("ctx", "split"), None, None),
            P(None, ("ctx", "split"), None, None),
            P(),
            P(),
            P("ctx", None, None, None),
        ),
        out_specs=P("ctx", None, None, None),
        check_vma=False,
    )
```

```python
import functools

import jax
import jax.numpy as jnp
from jax import lax
from jax.experimental import pallas as pl
from jax.experimental.pallas import tpu as pltpu
from jax.sharding import PartitionSpec as P

NEG = -1e30

PAGE = 64
HEAD = 128
TAIL = 8
ROWS = 2 * PAGE + TAIL
MiB = 1024 * 1024


def pack_kernel(
    page_ref,
    counts_ref,
    listed_ref,
    keys_ref,
    values_ref,
    out_ref,
    cache,
    message,
    count_here,
    listed,
    got,
    sent,
    small,
):
    items = out_ref.shape[0]
    page = page_ref[0]
    kv_heads = 4
    block = 8
    groups = items // block

    def fetch(g):
        at = pl.ds(g * block, block)
        return [
            pltpu.make_async_copy(ref.at[at], cache.at[at, a], got.at[a, g])
            for a, ref in enumerate((keys_ref, values_ref))
        ]

    def send(g):
        at = pl.ds(g * block, block)
        return pltpu.make_async_copy(message.at[at], out_ref.at[at], sent.at[g])

    columns = pl.ds(pl.multiple_of((page // HEAD) * HEAD, HEAD), HEAD)
    lists = pltpu.make_async_copy(listed_ref, listed, small.at[0])
    numbers = pltpu.make_async_copy(counts_ref.at[:, columns], count_here, small.at[1])
    lists.start()
    numbers.start()
    for g in range(groups):
        for copy in fetch(g):
            copy.start()
    lists.wait()
    second = jnp.max(jnp.where(listed[...] == page + 1, 1.0, 0.0), axis=1, keepdims=True)
    numbers.wait()
    row = lax.broadcasted_iota(jnp.int32, (16, 4 * PAGE), 0)
    slot = lax.broadcasted_iota(jnp.int32, (16, 4 * PAGE), 1)
    quarter = slot // PAGE
    slot = slot % PAGE
    out_row = lax.broadcasted_iota(jnp.int32, (16, HEAD), 0)
    for g in range(groups):
        for copy in fetch(g):
            copy.wait()
        for item in range(g * block, (g + 1) * block):
            if item % kv_heads == 0:
                request = item // kv_heads
                count = [count_here[request, page % HEAD + p] for p in range(2)]
                limit = jnp.where(row % 2 == 0, count[0], count[1])
                live = jnp.logical_and(quarter == row, slot < limit)
                live = jnp.where(live, 1.0, 0.0).astype(jnp.bfloat16)
                divisor = jnp.where(out_row % 2 == 0, count[0], count[1]).astype(jnp.float32)
                inverse = 1.0 / divisor
            choice = jnp.broadcast_to(second[item : item + 1, :], (PAGE, HEAD)) > 0.5
            for a in range(2):
                message[item, a * PAGE : (a + 1) * PAGE, :] = jnp.where(
                    choice, cache[item, a, 1], cache[item, a, 0]
                )
            both = cache[item].reshape(4 * PAGE, HEAD)
            total = jnp.dot(live, both, preferred_element_type=jnp.float32)
            message[item, 2 * PAGE : ROWS, :] = (total * inverse)[:TAIL].astype(jnp.bfloat16)
        send(g).start()
    for g in range(groups):
        send(g).wait()


def pack(page, counts, listed, cache_keys, cache_values):
    items = cache_keys.shape[0]
    groups = items // 8
    whole = pl.BlockSpec(memory_space=pl.ANY)
    return pl.pallas_call(
        pack_kernel,
        in_specs=[pl.BlockSpec(memory_space=pltpu.SMEM), whole, whole, whole, whole],
        out_specs=whole,
        out_shape=jax.ShapeDtypeStruct((items, ROWS, HEAD), jnp.bfloat16),
        scratch_shapes=[
            pltpu.VMEM((items, 2, 2, PAGE, HEAD), jnp.bfloat16),
            pltpu.VMEM((items, ROWS, HEAD), jnp.bfloat16),
            pltpu.SMEM((counts.shape[0], HEAD), jnp.int32),
            pltpu.VMEM(listed.shape, jnp.int32),
            pltpu.SemaphoreType.DMA((2, groups)),
            pltpu.SemaphoreType.DMA((groups,)),
            pltpu.SemaphoreType.DMA((2,)),
        ],
        compiler_params=pltpu.CompilerParams(vmem_limit_bytes=58 * MiB),
        name="pack",
    )(page, counts, listed, cache_keys, cache_values)


def split3(x):
    high = x.astype(jnp.bfloat16).astype(jnp.float32)
    rest = x - high
    middle = rest.astype(jnp.bfloat16).astype(jnp.float32)
    return high, middle, rest - middle


def attend_kernel(
    live_ref,
    cbias_ref,
    got_ref,
    q_ref,
    out_ref,
    keys,
    values,
    kt,
    vv,
    ckt,
    cv,
    cs0,
    cs1,
    sc0,
    sc1,
    best,
    top,
    acc,
    *,
    chunk,
    block,
    c,
):
    sources = got_ref.shape[0]
    cents = 2 * sources
    width = out_ref.shape[1] - 16
    blocks = q_ref.shape[0] // block
    sc, cs = (sc0, sc1), (cs0, cs1)

    tails = got_ref[:, 2 * PAGE : ROWS, :].astype(jnp.float32).reshape(sources * TAIL, HEAD)
    tails = tails.astype(jnp.bfloat16)
    r = lax.broadcasted_iota(jnp.int32, (cents, sources * TAIL), 0)
    col = lax.broadcasted_iota(jnp.int32, (cents, sources * TAIL), 1)
    first = (r // 2) * TAIL + r % 2
    cents_of = [
        jnp.dot(
            (col == first + off).astype(jnp.float32).astype(jnp.bfloat16),
            tails,
            preferred_element_type=jnp.float32,
        )
        for off in (0, 2)
    ]
    ckt[...] = jnp.transpose(cents_of[0]).astype(jnp.bfloat16)
    cv[:, :HEAD] = cents_of[1].astype(jnp.bfloat16)
    cv[:, HEAD:] = jnp.ones((cents, HEAD), jnp.bfloat16)

    def place(s, at):
        rows = pl.ds(at, PAGE)
        keys[rows, :] = got_ref[s, 0:PAGE, :].astype(jnp.float32)
        values[rows, :] = got_ref[s, PAGE : 2 * PAGE, :].astype(jnp.float32)
        return at + live_ref[s]

    end = lax.fori_loop(0, sources, place, 0, unroll=4)
    chunks = (end + chunk - 1) // chunk
    rest = pl.ds(end, chunk)
    keys[rest, :] = jnp.broadcast_to(keys[0:1, :], (chunk, HEAD))
    values[rest, :] = jnp.zeros((chunk, HEAD), jnp.float32)
    number = lax.broadcasted_iota(jnp.int32, (HEAD, HEAD), 0)

    def turn(j, carry):
        for k in range(0, chunk, HEAD):
            start = pl.multiple_of(j * chunk + k, HEAD)
            at = pl.ds(start, HEAD)
            kt[:, at] = jnp.transpose(keys[at, :]).astype(jnp.bfloat16)
            vv[at, :HEAD] = values[at, :].astype(jnp.bfloat16)
            vv[at, HEAD:] = jnp.where(number + start < end, 1.0, 0.0).astype(jnp.bfloat16)
        return carry

    lax.fori_loop(0, chunks, turn, 0)

    lanes = lax.broadcasted_iota(jnp.int32, (block, HEAD), 1)
    for b in range(blocks + 1):
        if b < blocks:
            rows = q_ref[b * block : (b + 1) * block, :]
            score = jnp.dot(rows, ckt[...], preferred_element_type=jnp.float32) + cbias_ref[...]
            cs[b % 2][...] = score
            best[...] = score
        if b > 0:
            weight = jnp.exp((cs[(b - 1) % 2][...] - top[...]) * c).astype(jnp.bfloat16)
            acc[...] = jnp.dot(weight, cv[...], preferred_element_type=jnp.float32)

        def body(j, carry, b=b):
            at = pl.ds(pl.multiple_of(j * chunk, chunk), chunk)
            if b > 0:
                tops = jnp.concatenate([top[...]] * (chunk // HEAD), axis=1)
                weight = jnp.exp((sc[(b - 1) % 2][:, at] - tops) * c).astype(jnp.bfloat16)
                half = chunk // 2
                for k in range(2):
                    at_k = pl.ds(pl.multiple_of(j * chunk + k * half, half), half)
                    acc[...] += jnp.dot(
                        weight[:, k * half : (k + 1) * half],
                        vv[at_k, :],
                        preferred_element_type=jnp.float32,
                    )
            if b < blocks:
                rows = q_ref[b * block : (b + 1) * block, :]
                score = jnp.dot(rows, kt[:, at], preferred_element_type=jnp.float32)
                sc[b % 2][:, at] = score
                parts = [score[:, k : k + HEAD] for k in range(0, chunk, HEAD)]
                best[...] = jnp.maximum(best[...], functools.reduce(jnp.maximum, parts))
            return carry

        lax.fori_loop(0, chunks, body, 0)
        if b > 0:
            total = acc[:, HEAD:]
            out = (acc[:, :HEAD] / total).astype(jnp.bfloat16)
            stats = jnp.transpose(jnp.where(lanes == 0, top[...], total))
            pieces = split3(stats[0:1, :]) + split3(stats[1:2, :])
            row = lax.broadcasted_iota(jnp.int32, (16, HEAD), 0)
            for k in range(block // width):
                to = (b - 1) * (block // width) + k
                out_ref[to, :width, :] = out[k * width : (k + 1) * width, :]
                tile = jnp.zeros((16, HEAD), jnp.float32)
                for i, piece in enumerate(pieces):
                    for h in range(2):
                        from_ = k * width + h * HEAD
                        tile = jnp.where(row == 2 * i + h, piece[:, from_ : from_ + HEAD], tile)
                out_ref[to, width:, :] = tile.astype(jnp.bfloat16)
        if b < blocks:
            top[...] = jnp.broadcast_to(jnp.max(best[...], axis=1, keepdims=True), (block, HEAD))


def attend(live, cbias, got, rows, parts, c):
    sources = got.shape[0]
    chunk = 512
    block = 512
    slots = sources * PAGE
    cents = 2 * sources
    width = rows.shape[0] // parts
    vmem = pl.BlockSpec(memory_space=pltpu.VMEM)
    return pl.pallas_call(
        functools.partial(attend_kernel, chunk=chunk, block=block, c=c),
        in_specs=[pl.BlockSpec(memory_space=pltpu.SMEM), vmem, vmem, vmem],
        out_specs=vmem,
        scratch_shapes=[
            pltpu.VMEM((slots + chunk, HEAD), jnp.float32),
            pltpu.VMEM((slots + chunk, HEAD), jnp.float32),
            pltpu.VMEM((HEAD, slots), jnp.bfloat16),
            pltpu.VMEM((slots, 2 * HEAD), jnp.bfloat16),
            pltpu.VMEM((HEAD, cents), jnp.bfloat16),
            pltpu.VMEM((cents, 2 * HEAD), jnp.bfloat16),
            pltpu.VMEM((block, cents), jnp.float32),
            pltpu.VMEM((block, cents), jnp.float32),
            pltpu.VMEM((block, slots), jnp.float32),
            pltpu.VMEM((block, slots), jnp.float32),
            pltpu.VMEM((block, HEAD), jnp.float32),
            pltpu.VMEM((block, HEAD), jnp.float32),
            pltpu.VMEM((block, 2 * HEAD), jnp.float32),
        ],
        out_shape=jax.ShapeDtypeStruct((parts, width + 16, HEAD), jnp.bfloat16),
        compiler_params=pltpu.CompilerParams(vmem_limit_bytes=40 * MiB),
        cost_estimate=pl.CostEstimate(
            flops=4 * rows.shape[0] * (slots + cents) * HEAD,
            bytes_accessed=4 * MiB,
            transcendentals=rows.shape[0] * (slots + cents),
        ),
        name="attend",
    )(live, cbias, got, rows)


def merge_kernel(got_ref, out_ref, *, c):
    parts = got_ref.shape[0]
    block = out_ref.shape[1]
    tops, totals = [], []
    for z in range(parts):
        tile = got_ref[z, block:, :].astype(jnp.float32)
        tops.append(tile[0:2] + tile[2:4] + tile[4:6])
        totals.append(tile[6:8] + tile[8:10] + tile[10:12])
    top = functools.reduce(jnp.maximum, tops)
    factors = [t * jnp.exp((m - top) * c) for m, t in zip(tops, totals)]
    whole = functools.reduce(jnp.add, factors)
    columns = jnp.transpose(jnp.concatenate([f / whole for f in factors], axis=0))
    for h in range(2):
        at = slice(h * HEAD, (h + 1) * HEAD)
        out = jnp.zeros((HEAD, HEAD), jnp.float32)
        for z in range(parts):
            column = columns[:, 2 * z + h : 2 * z + h + 1]
            out += got_ref[z, at, :].astype(jnp.float32) * column
        out = out.astype(jnp.bfloat16)
        for z in range(parts):
            out_ref[z, at, :] = out


def merge(got, c):
    parts, block, unused = got.shape
    block -= 16
    return pl.pallas_call(
        functools.partial(merge_kernel, c=c),
        out_shape=jax.ShapeDtypeStruct((parts, block, HEAD), jnp.bfloat16),
        compiler_params=pltpu.CompilerParams(vmem_limit_bytes=16 * MiB),
        name="merge",
    )(got)


def local(cache_keys, cache_values, counts, listed, queries):
    ctx_n = lax.axis_size("ctx")
    split_n = lax.axis_size("split")
    items, pages_here, page_len, head = cache_keys.shape
    requests = counts.shape[0]
    kv_heads = items // requests
    root = head**0.5
    c = head**-0.5
    item = lax.axis_index("ctx")
    split_idx = lax.axis_index("split")
    first = (item * split_n + split_idx) * pages_here
    message = pack(first.reshape(1), counts, listed, cache_keys, cache_values)
    got = lax.all_to_all(message, "ctx", split_axis=0, concat_axis=0, tiled=True)

    sel_row = lax.dynamic_index_in_dim(listed, item, 0, keepdims=False)
    count_row = lax.dynamic_index_in_dim(counts, item // kv_heads, 0, keepdims=False)
    mine = count_row.reshape(ctx_n, split_n, pages_here)
    mine = lax.dynamic_index_in_dim(mine, split_idx, 1, keepdims=False)
    source = jnp.arange(ctx_n, dtype=jnp.int32)[:, None]
    candidate = (source * split_n + split_idx) * pages_here + jnp.arange(
        pages_here, dtype=jnp.int32
    )
    marks = jnp.any(sel_row[None, None, :] == candidate[:, :, None], axis=2)
    live = jnp.sum(jnp.where(marks, mine, 0), axis=1)
    cbias = jnp.where(marks, NEG, jnp.log(mine.astype(jnp.float32)) * root)
    rows = queries.reshape(-1, head)
    partial = attend(live, cbias.reshape(1, -1), got, rows, split_n, c)
    shared = lax.all_to_all(partial, "split", split_axis=0, concat_axis=0, tiled=True)
    out = lax.all_to_all(merge(shared, c), "split", split_axis=0, concat_axis=0, tiled=True)
    return out.astype(jnp.float32).reshape(queries.shape)


def solution(mesh):
    return jax.shard_map(
        local,
        mesh=mesh,
        in_specs=(
            P(None, ("ctx", "split"), None, None),
            P(None, ("ctx", "split"), None, None),
            P(),
            P(),
            P("ctx", None, None, None),
        ),
        out_specs=P("ctx", None, None, None),
        check_vma=False,
    )
```

```python
import functools

import jax
import jax.numpy as jnp
from jax import lax
from jax.experimental import pallas as pl
from jax.experimental.pallas import tpu as pltpu
from jax.sharding import PartitionSpec as P

NEG = -1e30
LOG2E = 1.4426950408889634

PAGE = 64
HEAD = 128
TAIL = 8
ROWS = 2 * PAGE + TAIL
MiB = 1024 * 1024


def pack_kernel(
    page_ref,
    counts_ref,
    listed_ref,
    keys_ref,
    values_ref,
    out_ref,
    cache,
    message,
    count_here,
    listed,
    got,
    sent,
    small,
):
    items = out_ref.shape[0]
    page = page_ref[0]
    kv_heads = 4
    block = 8
    groups = items // block

    def fetch(g):
        at = pl.ds(g * block, block)
        return [
            pltpu.make_async_copy(ref.at[at], cache.at[at, a], got.at[a, g])
            for a, ref in enumerate((keys_ref, values_ref))
        ]

    def send(g):
        at = pl.ds(g * block, block)
        return pltpu.make_async_copy(message.at[at], out_ref.at[at], sent.at[g])

    columns = pl.ds(pl.multiple_of((page // HEAD) * HEAD, HEAD), HEAD)
    lists = pltpu.make_async_copy(listed_ref, listed, small.at[0])
    numbers = pltpu.make_async_copy(counts_ref.at[:, columns], count_here, small.at[1])
    lists.start()
    numbers.start()
    for g in range(groups):
        for copy in fetch(g):
            copy.start()
    lists.wait()
    second = jnp.max(jnp.where(listed[...] == page + 1, 1.0, 0.0), axis=1, keepdims=True)
    numbers.wait()
    row = lax.broadcasted_iota(jnp.int32, (16, 4 * PAGE), 0)
    slot = lax.broadcasted_iota(jnp.int32, (16, 4 * PAGE), 1)
    quarter = slot // PAGE
    slot = slot % PAGE
    out_row = lax.broadcasted_iota(jnp.int32, (16, HEAD), 0)
    for g in range(groups):
        for copy in fetch(g):
            copy.wait()
        for item in range(g * block, (g + 1) * block):
            if item % kv_heads == 0:
                request = item // kv_heads
                count = [count_here[request, page % HEAD + p] for p in range(2)]
                limit = jnp.where(row % 2 == 0, count[0], count[1])
                live = jnp.logical_and(quarter == row, slot < limit)
                live = jnp.where(live, 1.0, 0.0).astype(jnp.bfloat16)
                divisor = jnp.where(out_row % 2 == 0, count[0], count[1]).astype(jnp.float32)
                inverse = 1.0 / divisor
            choice = jnp.broadcast_to(second[item : item + 1, :], (PAGE, HEAD)) > 0.5
            for a in range(2):
                message[item, a * PAGE : (a + 1) * PAGE, :] = jnp.where(
                    choice, cache[item, a, 1], cache[item, a, 0]
                )
            both = cache[item].reshape(4 * PAGE, HEAD)
            total = jnp.dot(live, both, preferred_element_type=jnp.float32)
            message[item, 2 * PAGE : ROWS, :] = (total * inverse)[:TAIL].astype(jnp.bfloat16)
        send(g).start()
    for g in range(groups):
        send(g).wait()


def pack(page, counts, listed, cache_keys, cache_values):
    items = cache_keys.shape[0]
    groups = items // 8
    whole = pl.BlockSpec(memory_space=pl.ANY)
    return pl.pallas_call(
        pack_kernel,
        in_specs=[pl.BlockSpec(memory_space=pltpu.SMEM), whole, whole, whole, whole],
        out_specs=whole,
        out_shape=jax.ShapeDtypeStruct((items, ROWS, HEAD), jnp.bfloat16),
        scratch_shapes=[
            pltpu.VMEM((items, 2, 2, PAGE, HEAD), jnp.bfloat16),
            pltpu.VMEM((items, ROWS, HEAD), jnp.bfloat16),
            pltpu.SMEM((counts.shape[0], HEAD), jnp.int32),
            pltpu.VMEM(listed.shape, jnp.int32),
            pltpu.SemaphoreType.DMA((2, groups)),
            pltpu.SemaphoreType.DMA((groups,)),
            pltpu.SemaphoreType.DMA((2,)),
        ],
        compiler_params=pltpu.CompilerParams(vmem_limit_bytes=58 * MiB),
        name="pack",
    )(page, counts, listed, cache_keys, cache_values)


def split3(x):
    high = x.astype(jnp.bfloat16).astype(jnp.float32)
    rest = x - high
    middle = rest.astype(jnp.bfloat16).astype(jnp.float32)
    return high, middle, rest - middle


def store_scaled(ref, at, x):
    high = x.astype(jnp.bfloat16)
    ref[:HEAD, at] = high
    ref[HEAD:, at] = (x - high.astype(jnp.float32)).astype(jnp.bfloat16)


def attend_kernel(
    live_ref,
    cbias_ref,
    got_ref,
    q_ref,
    out_ref,
    keys,
    values,
    kt,
    vv,
    ckt,
    cv,
    qq,
    cs0,
    cs1,
    sc0,
    sc1,
    best,
    top,
    acc,
    *,
    chunk,
    block,
    c,
):
    sources = got_ref.shape[0]
    cents = 2 * sources
    width = out_ref.shape[1] - 16
    blocks = q_ref.shape[0] // block
    sc, cs = (sc0, sc1), (cs0, cs1)

    tails = got_ref[:, 2 * PAGE : ROWS, :].astype(jnp.float32).reshape(sources * TAIL, HEAD)
    tails = tails.astype(jnp.bfloat16)
    r = lax.broadcasted_iota(jnp.int32, (cents, sources * TAIL), 0)
    col = lax.broadcasted_iota(jnp.int32, (cents, sources * TAIL), 1)
    first = (r // 2) * TAIL + r % 2
    cents_of = [
        jnp.dot(
            (col == first + off).astype(jnp.float32).astype(jnp.bfloat16),
            tails,
            preferred_element_type=jnp.float32,
        )
        for off in (0, 2)
    ]
    store_scaled(ckt, slice(None), jnp.transpose(cents_of[0].astype(jnp.bfloat16).astype(jnp.float32)) * c)
    cv[:, :HEAD] = cents_of[1].astype(jnp.bfloat16)
    cv[:, HEAD:] = jnp.ones((cents, HEAD), jnp.bfloat16)

    def place(s, at):
        rows = pl.ds(at, PAGE)
        keys[rows, :] = got_ref[s, 0:PAGE, :].astype(jnp.float32)
        values[rows, :] = got_ref[s, PAGE : 2 * PAGE, :].astype(jnp.float32)
        return at + live_ref[s]

    end = lax.fori_loop(0, sources, place, 0, unroll=4)
    chunks = (end + chunk - 1) // chunk
    rest = pl.ds(end, chunk)
    keys[rest, :] = jnp.broadcast_to(keys[0:1, :], (chunk, HEAD))
    values[rest, :] = jnp.zeros((chunk, HEAD), jnp.float32)
    number = lax.broadcasted_iota(jnp.int32, (HEAD, HEAD), 0)

    def turn(j, carry):
        for k in range(0, chunk, HEAD):
            start = pl.multiple_of(j * chunk + k, HEAD)
            at = pl.ds(start, HEAD)
            store_scaled(kt, at, jnp.transpose(keys[at, :]) * c)
            vv[at, :HEAD] = values[at, :].astype(jnp.bfloat16)
            vv[at, HEAD:] = jnp.where(number + start < end, 1.0, 0.0).astype(jnp.bfloat16)
        return carry

    lax.fori_loop(0, chunks, turn, 0)

    lanes = lax.broadcasted_iota(jnp.int32, (block, HEAD), 1)
    for b in range(blocks + 1):
        if b < blocks:
            rows = q_ref[b * block : (b + 1) * block, :]
            qq[:, :HEAD] = rows
            qq[:, HEAD:] = rows
            score = jnp.dot(qq[...], ckt[...], preferred_element_type=jnp.float32) + cbias_ref[...]
            cs[b % 2][...] = score
            best[...] = score
        if b > 0:
            weight = jnp.exp2(cs[(b - 1) % 2][...] - top[...]).astype(jnp.bfloat16)
            acc[...] = jnp.dot(weight, cv[...], preferred_element_type=jnp.float32)

        def body(j, carry, b=b):
            at = pl.ds(pl.multiple_of(j * chunk, chunk), chunk)
            if b > 0:
                tops = jnp.concatenate([top[...]] * (chunk // HEAD), axis=1)
                weight = jnp.exp2(sc[(b - 1) % 2][:, at] - tops).astype(jnp.bfloat16)
                acc[...] += jnp.dot(weight, vv[at, :], preferred_element_type=jnp.float32)
            if b < blocks:
                score = jnp.dot(qq[...], kt[:, at], preferred_element_type=jnp.float32)
                sc[b % 2][:, at] = score
                parts = [score[:, k : k + HEAD] for k in range(0, chunk, HEAD)]
                best[...] = jnp.maximum(best[...], functools.reduce(jnp.maximum, parts))
            return carry

        lax.fori_loop(0, chunks, body, 0)
        if b > 0:
            total = acc[:, HEAD:]
            out = (acc[:, :HEAD] / total).astype(jnp.bfloat16)
            stats = jnp.transpose(jnp.where(lanes == 0, top[...], total))
            pieces = split3(stats[0:1, :]) + split3(stats[1:2, :])
            row = lax.broadcasted_iota(jnp.int32, (16, HEAD), 0)
            for k in range(block // width):
                to = (b - 1) * (block // width) + k
                out_ref[to, :width, :] = out[k * width : (k + 1) * width, :]
                tile = jnp.zeros((16, HEAD), jnp.float32)
                for i, piece in enumerate(pieces):
                    for h in range(2):
                        from_ = k * width + h * HEAD
                        tile = jnp.where(row == 2 * i + h, piece[:, from_ : from_ + HEAD], tile)
                out_ref[to, width:, :] = tile.astype(jnp.bfloat16)
        if b < blocks:
            top[...] = jnp.broadcast_to(jnp.max(best[...], axis=1, keepdims=True), (block, HEAD))


def attend(live, cbias, got, rows, parts, c):
    sources = got.shape[0]
    chunk = 512
    block = 512
    slots = sources * PAGE
    cents = 2 * sources
    width = rows.shape[0] // parts
    vmem = pl.BlockSpec(memory_space=pltpu.VMEM)
    return pl.pallas_call(
        functools.partial(attend_kernel, chunk=chunk, block=block, c=c),
        in_specs=[pl.BlockSpec(memory_space=pltpu.SMEM), vmem, vmem, vmem],
        out_specs=vmem,
        scratch_shapes=[
            pltpu.VMEM((slots + chunk, HEAD), jnp.float32),
            pltpu.VMEM((slots + chunk, HEAD), jnp.float32),
            pltpu.VMEM((2 * HEAD, slots), jnp.bfloat16),
            pltpu.VMEM((slots, 2 * HEAD), jnp.bfloat16),
            pltpu.VMEM((2 * HEAD, cents), jnp.bfloat16),
            pltpu.VMEM((cents, 2 * HEAD), jnp.bfloat16),
            pltpu.VMEM((block, 2 * HEAD), jnp.bfloat16),
            pltpu.VMEM((block, cents), jnp.float32),
            pltpu.VMEM((block, cents), jnp.float32),
            pltpu.VMEM((block, slots), jnp.float32),
            pltpu.VMEM((block, slots), jnp.float32),
            pltpu.VMEM((block, HEAD), jnp.float32),
            pltpu.VMEM((block, HEAD), jnp.float32),
            pltpu.VMEM((block, 2 * HEAD), jnp.float32),
        ],
        out_shape=jax.ShapeDtypeStruct((parts, width + 16, HEAD), jnp.bfloat16),
        compiler_params=pltpu.CompilerParams(vmem_limit_bytes=40 * MiB),
        cost_estimate=pl.CostEstimate(
            flops=4 * rows.shape[0] * (slots + cents) * HEAD,
            bytes_accessed=4 * MiB,
            transcendentals=rows.shape[0] * (slots + cents),
        ),
        name="attend",
    )(live, cbias, got, rows)


def merge_kernel(got_ref, out_ref):
    parts = got_ref.shape[0]
    block = out_ref.shape[1]
    tops, totals = [], []
    for z in range(parts):
        tile = got_ref[z, block:, :].astype(jnp.float32)
        tops.append(tile[0:2] + tile[2:4] + tile[4:6])
        totals.append(tile[6:8] + tile[8:10] + tile[10:12])
    top = functools.reduce(jnp.maximum, tops)
    factors = [t * jnp.exp2(m - top) for m, t in zip(tops, totals)]
    whole = functools.reduce(jnp.add, factors)
    columns = jnp.transpose(jnp.concatenate([f / whole for f in factors], axis=0))
    for h in range(2):
        at = slice(h * HEAD, (h + 1) * HEAD)
        out = jnp.zeros((HEAD, HEAD), jnp.float32)
        for z in range(parts):
            column = columns[:, 2 * z + h : 2 * z + h + 1]
            out += got_ref[z, at, :].astype(jnp.float32) * column
        out = out.astype(jnp.bfloat16)
        for z in range(parts):
            out_ref[z, at, :] = out


def merge(got):
    parts, block, unused = got.shape
    block -= 16
    return pl.pallas_call(
        merge_kernel,
        out_shape=jax.ShapeDtypeStruct((parts, block, HEAD), jnp.bfloat16),
        compiler_params=pltpu.CompilerParams(vmem_limit_bytes=16 * MiB),
        name="merge",
    )(got)


def local(cache_keys, cache_values, counts, listed, queries):
    ctx_n = lax.axis_size("ctx")
    split_n = lax.axis_size("split")
    items, pages_here, page_len, head = cache_keys.shape
    requests = counts.shape[0]
    kv_heads = items // requests
    c = head**-0.5 * LOG2E
    item = lax.axis_index("ctx")
    split_idx = lax.axis_index("split")
    first = (item * split_n + split_idx) * pages_here
    message = pack(first.reshape(1), counts, listed, cache_keys, cache_values)
    got = lax.all_to_all(message, "ctx", split_axis=0, concat_axis=0, tiled=True)

    sel_row = lax.dynamic_index_in_dim(listed, item, 0, keepdims=False)
    count_row = lax.dynamic_index_in_dim(counts, item // kv_heads, 0, keepdims=False)
    mine = count_row.reshape(ctx_n, split_n, pages_here)
    mine = lax.dynamic_index_in_dim(mine, split_idx, 1, keepdims=False)
    source = jnp.arange(ctx_n, dtype=jnp.int32)[:, None]
    candidate = (source * split_n + split_idx) * pages_here + jnp.arange(
        pages_here, dtype=jnp.int32
    )
    marks = jnp.any(sel_row[None, None, :] == candidate[:, :, None], axis=2)
    live = jnp.sum(jnp.where(marks, mine, 0), axis=1)
    cbias = jnp.where(marks, NEG, jnp.log(mine.astype(jnp.float32)) * LOG2E)
    rows = queries.reshape(-1, head)
    partial = attend(live, cbias.reshape(1, -1), got, rows, split_n, c)
    shared = lax.all_to_all(partial, "split", split_axis=0, concat_axis=0, tiled=True)
    out = lax.all_to_all(merge(shared), "split", split_axis=0, concat_axis=0, tiled=True)
    return out.astype(jnp.float32).reshape(queries.shape)


def solution(mesh):
    return jax.shard_map(
        local,
        mesh=mesh,
        in_specs=(
            P(None, ("ctx", "split"), None, None),
            P(None, ("ctx", "split"), None, None),
            P(),
            P(),
            P("ctx", None, None, None),
        ),
        out_specs=P("ctx", None, None, None),
        check_vma=False,
    )
```

```python
import functools

import jax
import jax.numpy as jnp
from jax import lax
from jax.experimental import pallas as pl
from jax.experimental.pallas import tpu as pltpu
from jax.sharding import PartitionSpec as P

NEG = -1e30

PAGE = 64
HEAD = 128
TAIL = 8
ROWS = 2 * PAGE + TAIL
MiB = 1024 * 1024

RING = [3 * i % 8 for i in range(8)]
CTX = [(x * 8 + y) * 2 + core for core in range(2) for x in range(4) for y in RING]


def pack_kernel(
    page_ref,
    counts_ref,
    listed_ref,
    keys_ref,
    values_ref,
    out_ref,
    cache,
    message,
    count_here,
    listed,
    got,
    sent,
    small,
):
    items = out_ref.shape[0]
    page = page_ref[0]
    kv_heads = 4
    block = 8
    groups = items // block

    def fetch(g):
        at = pl.ds(g * block, block)
        return [
            pltpu.make_async_copy(ref.at[at], cache.at[at, a], got.at[a, g])
            for a, ref in enumerate((keys_ref, values_ref))
        ]

    def send(g):
        at = pl.ds(g * block, block)
        return pltpu.make_async_copy(message.at[at], out_ref.at[at], sent.at[g])

    columns = pl.ds(pl.multiple_of((page // HEAD) * HEAD, HEAD), HEAD)
    lists = pltpu.make_async_copy(listed_ref, listed, small.at[0])
    numbers = pltpu.make_async_copy(counts_ref.at[:, columns], count_here, small.at[1])
    lists.start()
    numbers.start()
    for g in range(groups):
        for copy in fetch(g):
            copy.start()
    lists.wait()
    second = jnp.max(jnp.where(listed[...] == page + 1, 1.0, 0.0), axis=1, keepdims=True)
    numbers.wait()
    row = lax.broadcasted_iota(jnp.int32, (16, 4 * PAGE), 0)
    slot = lax.broadcasted_iota(jnp.int32, (16, 4 * PAGE), 1)
    quarter = slot // PAGE
    slot = slot % PAGE
    out_row = lax.broadcasted_iota(jnp.int32, (16, HEAD), 0)
    ready = set()
    for g in range(groups):
        for copy in fetch(g):
            copy.wait()
        for item in range(g * block, (g + 1) * block):
            if item % kv_heads == 0:
                request = item // kv_heads
                count = [count_here[request, page % HEAD + p] for p in range(2)]
                limit = jnp.where(row % 2 == 0, count[0], count[1])
                live = jnp.logical_and(quarter == row, slot < limit)
                live = jnp.where(live, 1.0, 0.0).astype(jnp.bfloat16)
                divisor = jnp.where(out_row % 2 == 0, count[0], count[1]).astype(jnp.float32)
                inverse = 1.0 / divisor
            choice = jnp.broadcast_to(second[item : item + 1, :], (PAGE, HEAD)) > 0.5
            for a in range(2):
                message[CTX.index(item), a * PAGE : (a + 1) * PAGE, :] = jnp.where(
                    choice, cache[item, a, 1], cache[item, a, 0]
                )
            both = cache[item].reshape(4 * PAGE, HEAD)
            total = jnp.dot(live, both, preferred_element_type=jnp.float32)
            message[CTX.index(item), 2 * PAGE : ROWS, :] = (total * inverse)[:TAIL].astype(
                jnp.bfloat16
            )
            ready.add(CTX.index(item))
        for h in range(groups):
            if ready.issuperset(range(h * block, (h + 1) * block)):
                send(h).start()
                ready.difference_update(range(h * block, (h + 1) * block))
    for g in range(groups):
        send(g).wait()


def pack(page, counts, listed, cache_keys, cache_values):
    items = cache_keys.shape[0]
    groups = items // 8
    whole = pl.BlockSpec(memory_space=pl.ANY)
    return pl.pallas_call(
        pack_kernel,
        in_specs=[pl.BlockSpec(memory_space=pltpu.SMEM), whole, whole, whole, whole],
        out_specs=whole,
        out_shape=jax.ShapeDtypeStruct((items, ROWS, HEAD), jnp.bfloat16),
        scratch_shapes=[
            pltpu.VMEM((items, 2, 2, PAGE, HEAD), jnp.bfloat16),
            pltpu.VMEM((items, ROWS, HEAD), jnp.bfloat16),
            pltpu.SMEM((counts.shape[0], HEAD), jnp.int32),
            pltpu.VMEM(listed.shape, jnp.int32),
            pltpu.SemaphoreType.DMA((2, groups)),
            pltpu.SemaphoreType.DMA((groups,)),
            pltpu.SemaphoreType.DMA((2,)),
        ],
        compiler_params=pltpu.CompilerParams(vmem_limit_bytes=58 * MiB),
        name="pack",
    )(page, counts, listed, cache_keys, cache_values)


def split3(x):
    high = x.astype(jnp.bfloat16).astype(jnp.float32)
    rest = x - high
    middle = rest.astype(jnp.bfloat16).astype(jnp.float32)
    return high, middle, rest - middle


def attend_kernel(
    live_ref,
    cbias_ref,
    got_ref,
    q_ref,
    out_ref,
    keys,
    values,
    kt,
    vv,
    ckt,
    cv,
    cs0,
    cs1,
    sc0,
    sc1,
    best,
    top,
    acc,
    *,
    chunk,
    block,
    c,
):
    sources = got_ref.shape[0]
    cents = 2 * sources
    width = out_ref.shape[1] - 16
    blocks = q_ref.shape[0] // block
    sc, cs = (sc0, sc1), (cs0, cs1)

    tails = got_ref[:, 2 * PAGE : ROWS, :].astype(jnp.float32).reshape(sources * TAIL, HEAD)
    tails = tails.astype(jnp.bfloat16)
    r = lax.broadcasted_iota(jnp.int32, (cents, sources * TAIL), 0)
    col = lax.broadcasted_iota(jnp.int32, (cents, sources * TAIL), 1)
    first = (r // 2) * TAIL + r % 2
    cents_of = [
        jnp.dot(
            (col == first + off).astype(jnp.float32).astype(jnp.bfloat16),
            tails,
            preferred_element_type=jnp.float32,
        )
        for off in (0, 2)
    ]
    ckt[...] = jnp.transpose(cents_of[0]).astype(jnp.bfloat16)
    cv[:, :HEAD] = cents_of[1].astype(jnp.bfloat16)
    cv[:, HEAD:] = jnp.ones((cents, HEAD), jnp.bfloat16)

    def place(s, at):
        rows = pl.ds(at, PAGE)
        keys[rows, :] = got_ref[s, 0:PAGE, :].astype(jnp.float32)
        values[rows, :] = got_ref[s, PAGE : 2 * PAGE, :].astype(jnp.float32)
        return at + live_ref[s]

    end = lax.fori_loop(0, sources, place, 0, unroll=4)
    chunks = (end + chunk - 1) // chunk
    rest = pl.ds(end, chunk)
    keys[rest, :] = jnp.broadcast_to(keys[0:1, :], (chunk, HEAD))
    values[rest, :] = jnp.zeros((chunk, HEAD), jnp.float32)
    number = lax.broadcasted_iota(jnp.int32, (HEAD, HEAD), 0)

    def turn(j, carry):
        for k in range(0, chunk, HEAD):
            start = pl.multiple_of(j * chunk + k, HEAD)
            at = pl.ds(start, HEAD)
            kt[:, at] = jnp.transpose(keys[at, :]).astype(jnp.bfloat16)
            vv[at, :HEAD] = values[at, :].astype(jnp.bfloat16)
            vv[at, HEAD:] = jnp.where(number + start < end, 1.0, 0.0).astype(jnp.bfloat16)
        return carry

    lax.fori_loop(0, chunks, turn, 0)

    lanes = lax.broadcasted_iota(jnp.int32, (block, HEAD), 1)
    for b in range(blocks + 1):
        if b < blocks:
            rows = q_ref[b * block : (b + 1) * block, :]
            score = jnp.dot(rows, ckt[...], preferred_element_type=jnp.float32) + cbias_ref[...]
            cs[b % 2][...] = score
            best[...] = score
        if b > 0:
            weight = jnp.exp((cs[(b - 1) % 2][...] - top[...]) * c).astype(jnp.bfloat16)
            acc[...] = jnp.dot(weight, cv[...], preferred_element_type=jnp.float32)

        def body(j, carry, b=b):
            at = pl.ds(pl.multiple_of(j * chunk, chunk), chunk)
            if b > 0:
                tops = jnp.concatenate([top[...]] * (chunk // HEAD), axis=1)
                weight = jnp.exp((sc[(b - 1) % 2][:, at] - tops) * c).astype(jnp.bfloat16)
                half = chunk // 2
                for k in range(2):
                    at_k = pl.ds(pl.multiple_of(j * chunk + k * half, half), half)
                    acc[...] += jnp.dot(
                        weight[:, k * half : (k + 1) * half],
                        vv[at_k, :],
                        preferred_element_type=jnp.float32,
                    )
            if b < blocks:
                rows = q_ref[b * block : (b + 1) * block, :]
                score = jnp.dot(rows, kt[:, at], preferred_element_type=jnp.float32)
                sc[b % 2][:, at] = score
                parts = [score[:, k : k + HEAD] for k in range(0, chunk, HEAD)]
                best[...] = jnp.maximum(best[...], functools.reduce(jnp.maximum, parts))
            return carry

        lax.fori_loop(0, chunks, body, 0)
        if b > 0:
            total = acc[:, HEAD:]
            out = (acc[:, :HEAD] / total).astype(jnp.bfloat16)
            stats = jnp.transpose(jnp.where(lanes == 0, top[...], total))
            pieces = split3(stats[0:1, :]) + split3(stats[1:2, :])
            row = lax.broadcasted_iota(jnp.int32, (16, HEAD), 0)
            for k in range(block // width):
                to = RING.index((b - 1) * (block // width) + k)
                out_ref[to, :width, :] = out[k * width : (k + 1) * width, :]
                tile = jnp.zeros((16, HEAD), jnp.float32)
                for i, piece in enumerate(pieces):
                    for h in range(2):
                        from_ = k * width + h * HEAD
                        tile = jnp.where(row == 2 * i + h, piece[:, from_ : from_ + HEAD], tile)
                out_ref[to, width:, :] = tile.astype(jnp.bfloat16)
        if b < blocks:
            top[...] = jnp.broadcast_to(jnp.max(best[...], axis=1, keepdims=True), (block, HEAD))


def attend(live, cbias, got, rows, parts, c):
    sources = got.shape[0]
    chunk = 512
    block = 512
    slots = sources * PAGE
    cents = 2 * sources
    width = rows.shape[0] // parts
    vmem = pl.BlockSpec(memory_space=pltpu.VMEM)
    return pl.pallas_call(
        functools.partial(attend_kernel, chunk=chunk, block=block, c=c),
        in_specs=[pl.BlockSpec(memory_space=pltpu.SMEM), vmem, vmem, vmem],
        out_specs=vmem,
        scratch_shapes=[
            pltpu.VMEM((slots + chunk, HEAD), jnp.float32),
            pltpu.VMEM((slots + chunk, HEAD), jnp.float32),
            pltpu.VMEM((HEAD, slots), jnp.bfloat16),
            pltpu.VMEM((slots, 2 * HEAD), jnp.bfloat16),
            pltpu.VMEM((HEAD, cents), jnp.bfloat16),
            pltpu.VMEM((cents, 2 * HEAD), jnp.bfloat16),
            pltpu.VMEM((block, cents), jnp.float32),
            pltpu.VMEM((block, cents), jnp.float32),
            pltpu.VMEM((block, slots), jnp.float32),
            pltpu.VMEM((block, slots), jnp.float32),
            pltpu.VMEM((block, HEAD), jnp.float32),
            pltpu.VMEM((block, HEAD), jnp.float32),
            pltpu.VMEM((block, 2 * HEAD), jnp.float32),
        ],
        out_shape=jax.ShapeDtypeStruct((parts, width + 16, HEAD), jnp.bfloat16),
        compiler_params=pltpu.CompilerParams(vmem_limit_bytes=40 * MiB),
        cost_estimate=pl.CostEstimate(
            flops=4 * rows.shape[0] * (slots + cents) * HEAD,
            bytes_accessed=4 * MiB,
            transcendentals=rows.shape[0] * (slots + cents),
        ),
        name="attend",
    )(live, cbias, got, rows)


def merge_kernel(got_ref, out_ref, *, c):
    parts = got_ref.shape[0]
    block = out_ref.shape[1]
    tops, totals = [], []
    for z in range(parts):
        tile = got_ref[z, block:, :].astype(jnp.float32)
        tops.append(tile[0:2] + tile[2:4] + tile[4:6])
        totals.append(tile[6:8] + tile[8:10] + tile[10:12])
    top = functools.reduce(jnp.maximum, tops)
    factors = [t * jnp.exp((m - top) * c) for m, t in zip(tops, totals)]
    whole = functools.reduce(jnp.add, factors)
    columns = jnp.transpose(jnp.concatenate([f / whole for f in factors], axis=0))
    for h in range(2):
        at = slice(h * HEAD, (h + 1) * HEAD)
        out = jnp.zeros((HEAD, HEAD), jnp.float32)
        for z in range(parts):
            column = columns[:, 2 * z + h : 2 * z + h + 1]
            out += got_ref[z, at, :].astype(jnp.float32) * column
        out = out.astype(jnp.bfloat16)
        for z in range(parts):
            out_ref[z, at, :] = out


def merge(got, c):
    parts, block, unused = got.shape
    block -= 16
    return pl.pallas_call(
        functools.partial(merge_kernel, c=c),
        out_shape=jax.ShapeDtypeStruct((parts, block, HEAD), jnp.bfloat16),
        compiler_params=pltpu.CompilerParams(vmem_limit_bytes=16 * MiB),
        name="merge",
    )(got)


def exchange(blocks, axis, order):
    return lax.all_to_all(
        blocks, axis, split_axis=0, concat_axis=0, axis_index_groups=[order], tiled=True
    )


def local(cache_keys, cache_values, counts, listed, queries):
    ctx_n = lax.axis_size("ctx")
    split_n = lax.axis_size("split")
    items, pages_here, page_len, head = cache_keys.shape
    requests = counts.shape[0]
    kv_heads = items // requests
    root = head**0.5
    c = head**-0.5
    item = lax.axis_index("ctx")
    split_idx = lax.axis_index("split")
    first = (item * split_n + split_idx) * pages_here
    message = pack(first.reshape(1), counts, listed, cache_keys, cache_values)
    got = exchange(message, "ctx", CTX)

    sel_row = lax.dynamic_index_in_dim(listed, item, 0, keepdims=False)
    count_row = lax.dynamic_index_in_dim(counts, item // kv_heads, 0, keepdims=False)
    mine = count_row.reshape(ctx_n, split_n, pages_here)
    mine = lax.dynamic_index_in_dim(mine, split_idx, 1, keepdims=False)
    mine = mine.reshape(4, 8, 2, pages_here).transpose(2, 0, 1, 3)
    mine = jnp.stack([mine[:, :, y] for y in RING], axis=2).reshape(ctx_n, pages_here)
    source = jnp.array(CTX, jnp.int32)[:, None]
    candidate = (source * split_n + split_idx) * pages_here + jnp.arange(
        pages_here, dtype=jnp.int32
    )
    marks = jnp.any(sel_row[None, None, :] == candidate[:, :, None], axis=2)
    live = jnp.sum(jnp.where(marks, mine, 0), axis=1)
    cbias = jnp.where(marks, NEG, jnp.log(mine.astype(jnp.float32)) * root)
    rows = queries.reshape(-1, head)
    partial = attend(live, cbias.reshape(1, -1), got, rows, split_n, c)
    shared = exchange(partial, "split", RING)
    out = exchange(merge(shared, c), "split", RING)
    out = jnp.concatenate([out[RING.index(z)] for z in range(split_n)], axis=0)
    return out.astype(jnp.float32).reshape(queries.shape)


def solution(mesh):
    return jax.shard_map(
        local,
        mesh=mesh,
        in_specs=(
            P(None, ("ctx", "split"), None, None),
            P(None, ("ctx", "split"), None, None),
            P(),
            P(),
            P("ctx", None, None, None),
        ),
        out_specs=P("ctx", None, None, None),
        check_vma=False,
    )
```

```python
import functools

import jax
import jax.numpy as jnp
from jax import lax
from jax.experimental import pallas as pl
from jax.experimental.pallas import tpu as pltpu
from jax.sharding import PartitionSpec as P

NEG = -1e30

PAGE = 64
HEAD = 128
TAIL = 8
ROWS = 2 * PAGE + TAIL
MiB = 1024 * 1024

RING = [3 * i % 8 for i in range(8)]
CTX = [(x * 8 + y) * 2 + core for core in range(2) for x in range(4) for y in RING]


def pack_kernel(
    page_ref,
    counts_ref,
    listed_ref,
    keys_ref,
    values_ref,
    out_ref,
    cache,
    message,
    count_here,
    listed,
    got,
    sent,
    small,
):
    items = out_ref.shape[0]
    page = page_ref[0]
    kv_heads = 4
    block = 8
    groups = items // block

    def fetch(g):
        at = pl.ds(g * block, block)
        return [
            pltpu.make_async_copy(ref.at[at], cache.at[at, a], got.at[a, g])
            for a, ref in enumerate((keys_ref, values_ref))
        ]

    def send(g):
        at = pl.ds(g * block, block)
        return pltpu.make_async_copy(message.at[at], out_ref.at[at], sent.at[g])

    columns = pl.ds(pl.multiple_of((page // HEAD) * HEAD, HEAD), HEAD)
    lists = pltpu.make_async_copy(listed_ref, listed, small.at[0])
    numbers = pltpu.make_async_copy(counts_ref.at[:, columns], count_here, small.at[1])
    lists.start()
    numbers.start()
    for g in range(groups):
        for copy in fetch(g):
            copy.start()
    lists.wait()
    second = jnp.max(jnp.where(listed[...] == page + 1, 1.0, 0.0), axis=1, keepdims=True)
    numbers.wait()
    row = lax.broadcasted_iota(jnp.int32, (16, 4 * PAGE), 0)
    slot = lax.broadcasted_iota(jnp.int32, (16, 4 * PAGE), 1)
    quarter = slot // PAGE
    slot = slot % PAGE
    out_row = lax.broadcasted_iota(jnp.int32, (16, HEAD), 0)
    ready = set()
    for g in range(groups):
        for copy in fetch(g):
            copy.wait()
        for item in range(g * block, (g + 1) * block):
            if item % kv_heads == 0:
                request = item // kv_heads
                count = [count_here[request, page % HEAD + p] for p in range(2)]
                limit = jnp.where(row % 2 == 0, count[0], count[1])
                live = jnp.logical_and(quarter == row, slot < limit)
                live = jnp.where(live, 1.0, 0.0).astype(jnp.bfloat16)
                divisor = jnp.where(out_row % 2 == 0, count[0], count[1]).astype(jnp.float32)
                inverse = 1.0 / divisor
            choice = jnp.broadcast_to(second[item : item + 1, :], (PAGE, HEAD)) > 0.5
            for a in range(2):
                message[CTX.index(item), a * PAGE : (a + 1) * PAGE, :] = jnp.where(
                    choice, cache[item, a, 1], cache[item, a, 0]
                )
            both = cache[item].reshape(4 * PAGE, HEAD)
            total = jnp.dot(live, both, preferred_element_type=jnp.float32)
            message[CTX.index(item), 2 * PAGE : ROWS, :] = (total * inverse)[:TAIL].astype(
                jnp.bfloat16
            )
            ready.add(CTX.index(item))
        for h in range(groups):
            if ready.issuperset(range(h * block, (h + 1) * block)):
                send(h).start()
                ready.difference_update(range(h * block, (h + 1) * block))
    for g in range(groups):
        send(g).wait()


def pack(page, counts, listed, cache_keys, cache_values):
    items = cache_keys.shape[0]
    groups = items // 8
    whole = pl.BlockSpec(memory_space=pl.ANY)
    return pl.pallas_call(
        pack_kernel,
        in_specs=[pl.BlockSpec(memory_space=pltpu.SMEM), whole, whole, whole, whole],
        out_specs=whole,
        out_shape=jax.ShapeDtypeStruct((items, ROWS, HEAD), jnp.bfloat16),
        scratch_shapes=[
            pltpu.VMEM((items, 2, 2, PAGE, HEAD), jnp.bfloat16),
            pltpu.VMEM((items, ROWS, HEAD), jnp.bfloat16),
            pltpu.SMEM((counts.shape[0], HEAD), jnp.int32),
            pltpu.VMEM(listed.shape, jnp.int32),
            pltpu.SemaphoreType.DMA((2, groups)),
            pltpu.SemaphoreType.DMA((groups,)),
            pltpu.SemaphoreType.DMA((2,)),
        ],
        compiler_params=pltpu.CompilerParams(vmem_limit_bytes=58 * MiB),
        name="pack",
    )(page, counts, listed, cache_keys, cache_values)


def split3(x):
    high = x.astype(jnp.bfloat16).astype(jnp.float32)
    rest = x - high
    middle = rest.astype(jnp.bfloat16).astype(jnp.float32)
    return high, middle, rest - middle


def attend_kernel(
    live_ref,
    cbias_ref,
    got_ref,
    q_ref,
    out_ref,
    keys,
    values,
    kt,
    vv,
    ckt,
    cv,
    cs,
    sc,
    best,
    top,
    acc,
    *,
    chunk,
    c,
):
    sources = got_ref.shape[0]
    cents = 2 * sources
    width = out_ref.shape[1] - 16
    block = sc.shape[0]

    tails = got_ref[:, 2 * PAGE : ROWS, :].astype(jnp.float32).reshape(sources * TAIL, HEAD)
    tails = tails.astype(jnp.bfloat16)
    r = lax.broadcasted_iota(jnp.int32, (cents, sources * TAIL), 0)
    col = lax.broadcasted_iota(jnp.int32, (cents, sources * TAIL), 1)
    first = (r // 2) * TAIL + r % 2
    cents_of = [
        jnp.dot(
            (col == first + off).astype(jnp.float32).astype(jnp.bfloat16),
            tails,
            preferred_element_type=jnp.float32,
        )
        for off in (0, 2)
    ]
    ckt[...] = jnp.transpose(cents_of[0]).astype(jnp.bfloat16)
    cv[:, :HEAD] = cents_of[1].astype(jnp.bfloat16)
    cv[:, HEAD:] = jnp.ones((cents, HEAD), jnp.bfloat16)

    def place(s, at):
        rows = pl.ds(at, PAGE)
        keys[rows, :] = got_ref[s, 0:PAGE, :].astype(jnp.float32)
        values[rows, :] = got_ref[s, PAGE : 2 * PAGE, :].astype(jnp.float32)
        return at + live_ref[s]

    end = lax.fori_loop(0, sources, place, 0, unroll=4)
    chunks = (end + chunk - 1) // chunk
    rest = pl.ds(end, chunk)
    keys[rest, :] = jnp.broadcast_to(keys[0:1, :], (chunk, HEAD))
    values[rest, :] = jnp.zeros((chunk, HEAD), jnp.float32)
    number = lax.broadcasted_iota(jnp.int32, (HEAD, HEAD), 0)

    def turn(j, carry):
        for k in range(0, chunk, HEAD):
            start = pl.multiple_of(j * chunk + k, HEAD)
            at = pl.ds(start, HEAD)
            kt[:, at] = jnp.transpose(keys[at, :]).astype(jnp.bfloat16)
            vv[at, :HEAD] = values[at, :].astype(jnp.bfloat16)
            vv[at, HEAD:] = jnp.where(number + start < end, 1.0, 0.0).astype(jnp.bfloat16)
        return carry

    lax.fori_loop(0, chunks, turn, 0)

    for first in range(0, q_ref.shape[0], block):
        score = jnp.dot(q_ref[first : first + block, :], ckt[...], preferred_element_type=jnp.float32) + cbias_ref[...]
        cs[...] = score
        best[...] = score

        def scores(j, carry):
            at = pl.ds(pl.multiple_of(j * chunk, chunk), chunk)
            score = jnp.dot(q_ref[first : first + block, :], kt[:, at], preferred_element_type=jnp.float32)
            sc[:, at] = score
            parts = [score[:, k : k + HEAD] for k in range(0, chunk, HEAD)]
            best[...] = jnp.maximum(best[...], functools.reduce(jnp.maximum, parts))
            return carry

        lax.fori_loop(0, chunks, scores, 0)
        top[...] = jnp.broadcast_to(jnp.max(best[...], axis=1, keepdims=True), (block, HEAD))
        weight = jnp.exp((cs[...] - top[...]) * c).astype(jnp.bfloat16)
        acc[...] = jnp.dot(weight, cv[...], preferred_element_type=jnp.float32)

        def weighted(j, carry):
            at = pl.ds(pl.multiple_of(j * chunk, chunk), chunk)
            tops = jnp.concatenate([top[...]] * (chunk // HEAD), axis=1)
            weight = jnp.exp((sc[:, at] - tops) * c).astype(jnp.bfloat16)
            acc[...] += jnp.dot(weight, vv[at, :], preferred_element_type=jnp.float32)
            return carry

        lax.fori_loop(0, chunks, weighted, 0)
        lanes = lax.broadcasted_iota(jnp.int32, (width, HEAD), 1)
        row = lax.broadcasted_iota(jnp.int32, (16, HEAD), 0)
        for z in range(block // width):
            at = slice(z * width, (z + 1) * width)
            to = RING.index(first // width + z)
            total = acc[at, HEAD:]
            out_ref[to, :width, :] = (acc[at, :HEAD] / total).astype(jnp.bfloat16)
            stats = jnp.transpose(jnp.where(lanes == 0, top[at, :], total))
            tile = jnp.zeros((16, HEAD), jnp.float32)
            for i, piece in enumerate(split3(stats[0:1, :]) + split3(stats[1:2, :])):
                for h in range(2):
                    tile = jnp.where(row == 2 * i + h, piece[:, h * HEAD : (h + 1) * HEAD], tile)
            out_ref[to, width:, :] = tile.astype(jnp.bfloat16)


def attend(live, cbias, got, rows, parts, c):
    sources = got.shape[0]
    chunk = 512
    block = rows.shape[0] // 2
    slots = sources * PAGE
    cents = 2 * sources
    width = rows.shape[0] // parts
    vmem = pl.BlockSpec(memory_space=pltpu.VMEM)
    return pl.pallas_call(
        functools.partial(attend_kernel, chunk=chunk, c=c),
        in_specs=[pl.BlockSpec(memory_space=pltpu.SMEM), vmem, vmem, vmem],
        out_specs=vmem,
        scratch_shapes=[
            pltpu.VMEM((slots + chunk, HEAD), jnp.float32),
            pltpu.VMEM((slots + chunk, HEAD), jnp.float32),
            pltpu.VMEM((HEAD, slots), jnp.bfloat16),
            pltpu.VMEM((slots, 2 * HEAD), jnp.bfloat16),
            pltpu.VMEM((HEAD, cents), jnp.bfloat16),
            pltpu.VMEM((cents, 2 * HEAD), jnp.bfloat16),
            pltpu.VMEM((block, cents), jnp.float32),
            pltpu.VMEM((block, slots), jnp.float32),
            pltpu.VMEM((block, HEAD), jnp.float32),
            pltpu.VMEM((block, HEAD), jnp.float32),
            pltpu.VMEM((block, 2 * HEAD), jnp.float32),
        ],
        out_shape=jax.ShapeDtypeStruct((parts, width + 16, HEAD), jnp.bfloat16),
        compiler_params=pltpu.CompilerParams(vmem_limit_bytes=40 * MiB),
        cost_estimate=pl.CostEstimate(
            flops=4 * rows.shape[0] * (slots + cents) * HEAD,
            bytes_accessed=4 * MiB,
            transcendentals=rows.shape[0] * (slots + cents),
        ),
        name="attend",
    )(live, cbias, got, rows)


def merge_kernel(got_ref, out_ref, *, c):
    parts = got_ref.shape[0]
    block = out_ref.shape[1]
    tops, totals = [], []
    for z in range(parts):
        tile = got_ref[z, block:, :].astype(jnp.float32)
        tops.append(tile[0:2] + tile[2:4] + tile[4:6])
        totals.append(tile[6:8] + tile[8:10] + tile[10:12])
    top = functools.reduce(jnp.maximum, tops)
    factors = [t * jnp.exp((m - top) * c) for m, t in zip(tops, totals)]
    whole = functools.reduce(jnp.add, factors)
    columns = jnp.transpose(jnp.concatenate([f / whole for f in factors], axis=0))
    for h in range(2):
        at = slice(h * HEAD, (h + 1) * HEAD)
        out = jnp.zeros((HEAD, HEAD), jnp.float32)
        for z in range(parts):
            column = columns[:, 2 * z + h : 2 * z + h + 1]
            out += got_ref[z, at, :].astype(jnp.float32) * column
        out = out.astype(jnp.bfloat16)
        for z in range(parts):
            out_ref[z, at, :] = out


def merge(got, c):
    parts, block, unused = got.shape
    block -= 16
    return pl.pallas_call(
        functools.partial(merge_kernel, c=c),
        out_shape=jax.ShapeDtypeStruct((parts, block, HEAD), jnp.bfloat16),
        compiler_params=pltpu.CompilerParams(vmem_limit_bytes=16 * MiB),
        name="merge",
    )(got)


def exchange(blocks, axis, order):
    return lax.all_to_all(
        blocks, axis, split_axis=0, concat_axis=0, axis_index_groups=[order], tiled=True
    )


def local(cache_keys, cache_values, counts, listed, queries):
    ctx_n = lax.axis_size("ctx")
    split_n = lax.axis_size("split")
    items, pages_here, page_len, head = cache_keys.shape
    requests = counts.shape[0]
    kv_heads = items // requests
    root = head**0.5
    c = head**-0.5
    item = lax.axis_index("ctx")
    split_idx = lax.axis_index("split")
    first = (item * split_n + split_idx) * pages_here
    message = pack(first.reshape(1), counts, listed, cache_keys, cache_values)
    got = exchange(message, "ctx", CTX)

    sel_row = lax.dynamic_index_in_dim(listed, item, 0, keepdims=False)
    count_row = lax.dynamic_index_in_dim(counts, item // kv_heads, 0, keepdims=False)
    mine = count_row.reshape(ctx_n, split_n, pages_here)
    mine = lax.dynamic_index_in_dim(mine, split_idx, 1, keepdims=False)
    mine = mine.reshape(4, 8, 2, pages_here).transpose(2, 0, 1, 3)
    mine = jnp.stack([mine[:, :, y] for y in RING], axis=2).reshape(ctx_n, pages_here)
    source = jnp.array(CTX, jnp.int32)[:, None]
    candidate = (source * split_n + split_idx) * pages_here + jnp.arange(
        pages_here, dtype=jnp.int32
    )
    marks = jnp.any(sel_row[None, None, :] == candidate[:, :, None], axis=2)
    live = jnp.sum(jnp.where(marks, mine, 0), axis=1)
    cbias = jnp.where(marks, NEG, jnp.log(mine.astype(jnp.float32)) * root)
    rows = queries.reshape(-1, head)
    partial = attend(live, cbias.reshape(1, -1), got, rows, split_n, c)
    shared = exchange(partial, "split", RING)
    out = exchange(merge(shared, c), "split", RING)
    out = jnp.concatenate([out[RING.index(z)] for z in range(split_n)], axis=0)
    return out.astype(jnp.float32).reshape(queries.shape)


def solution(mesh):
    return jax.shard_map(
        local,
        mesh=mesh,
        in_specs=(
            P(None, ("ctx", "split"), None, None),
            P(None, ("ctx", "split"), None, None),
            P(),
            P(),
            P("ctx", None, None, None),
        ),
        out_specs=P("ctx", None, None, None),
        check_vma=False,
    )
```

```python
import functools

import jax
import jax.numpy as jnp
from jax import lax
from jax.experimental import pallas as pl
from jax.experimental.pallas import tpu as pltpu
from jax.sharding import PartitionSpec as P

NEG = -1e30

PAGE = 64
HEAD = 128
TAIL = 8
ROWS = 2 * PAGE + TAIL
MiB = 1024 * 1024

RING = [3 * i % 8 for i in range(8)]
CTX = [(x * 8 + y) * 2 + core for core in range(2) for x in range(4) for y in RING]


def pack_kernel(
    page_ref,
    counts_ref,
    listed_ref,
    keys_ref,
    values_ref,
    out_ref,
    cache,
    message,
    count_here,
    listed,
    got,
    sent,
    small,
):
    items = out_ref.shape[0]
    page = page_ref[0]
    kv_heads = 4
    block = 8
    groups = items // block

    def fetch(g):
        at = pl.ds(g * block, block)
        return [
            pltpu.make_async_copy(ref.at[at], cache.at[at, a], got.at[a, g])
            for a, ref in enumerate((keys_ref, values_ref))
        ]

    def send(g):
        at = pl.ds(g * block, block)
        return pltpu.make_async_copy(message.at[at], out_ref.at[at], sent.at[g])

    columns = pl.ds(pl.multiple_of((page // HEAD) * HEAD, HEAD), HEAD)
    lists = pltpu.make_async_copy(listed_ref, listed, small.at[0])
    numbers = pltpu.make_async_copy(counts_ref.at[:, columns], count_here, small.at[1])
    lists.start()
    numbers.start()
    for g in range(groups):
        for copy in fetch(g):
            copy.start()
    lists.wait()
    second = jnp.max(jnp.where(listed[...] == page + 1, 1.0, 0.0), axis=1, keepdims=True)
    numbers.wait()
    row = lax.broadcasted_iota(jnp.int32, (16, 4 * PAGE), 0)
    slot = lax.broadcasted_iota(jnp.int32, (16, 4 * PAGE), 1)
    quarter = slot // PAGE
    slot = slot % PAGE
    out_row = lax.broadcasted_iota(jnp.int32, (16, HEAD), 0)
    ready = set()
    for g in range(groups):
        for copy in fetch(g):
            copy.wait()
        for item in range(g * block, (g + 1) * block):
            to = CTX.index(item)
            choice = jnp.broadcast_to(second[item : item + 1, :], (PAGE, HEAD)) > 0.5
            for a in range(2):
                message[to, a * PAGE : (a + 1) * PAGE, :] = jnp.where(
                    choice, cache[item, a, 1], cache[item, a, 0]
                )
        for item in range(g * block, (g + 1) * block, 2):
            if item % kv_heads == 0:
                request = item // kv_heads
                count = [count_here[request, page % HEAD + p] for p in range(2)]
                limit = jnp.where(row % 2 == 0, count[0], count[1])
                live = jnp.logical_and(quarter == row, slot < limit)
                live = jnp.where(live, 1.0, 0.0).astype(jnp.bfloat16)
                divisor = jnp.where(out_row % 2 == 0, count[0], count[1]).astype(jnp.float32)
                inverse = 1.0 / divisor
            both = jnp.concatenate(
                [cache[i].reshape(4 * PAGE, HEAD) for i in (item, item + 1)], axis=1
            )
            total = jnp.dot(live, both, preferred_element_type=jnp.float32)
            for k in range(2):
                mean = total[:, k * HEAD : (k + 1) * HEAD] * inverse
                message[CTX.index(item + k), 2 * PAGE : ROWS, :] = mean[:TAIL].astype(jnp.bfloat16)
        ready.update(CTX.index(item) for item in range(g * block, (g + 1) * block))
        for h in range(groups):
            if ready.issuperset(range(h * block, (h + 1) * block)):
                send(h).start()
                ready.difference_update(range(h * block, (h + 1) * block))
    for g in range(groups):
        send(g).wait()


def pack(page, counts, listed, cache_keys, cache_values):
    items = cache_keys.shape[0]
    groups = items // 8
    whole = pl.BlockSpec(memory_space=pl.ANY)
    return pl.pallas_call(
        pack_kernel,
        in_specs=[pl.BlockSpec(memory_space=pltpu.SMEM), whole, whole, whole, whole],
        out_specs=whole,
        out_shape=jax.ShapeDtypeStruct((items, ROWS, HEAD), jnp.bfloat16),
        scratch_shapes=[
            pltpu.VMEM((items, 2, 2, PAGE, HEAD), jnp.bfloat16),
            pltpu.VMEM((items, ROWS, HEAD), jnp.bfloat16),
            pltpu.SMEM((counts.shape[0], HEAD), jnp.int32),
            pltpu.VMEM(listed.shape, jnp.int32),
            pltpu.SemaphoreType.DMA((2, groups)),
            pltpu.SemaphoreType.DMA((groups,)),
            pltpu.SemaphoreType.DMA((2,)),
        ],
        compiler_params=pltpu.CompilerParams(vmem_limit_bytes=58 * MiB),
        name="pack",
    )(page, counts, listed, cache_keys, cache_values)


def split3(x):
    high = x.astype(jnp.bfloat16).astype(jnp.float32)
    rest = x - high
    middle = rest.astype(jnp.bfloat16).astype(jnp.float32)
    return high, middle, rest - middle


def attend_kernel(
    live_ref,
    cbias_ref,
    got_ref,
    q_ref,
    out_ref,
    keys,
    values,
    kt,
    vv,
    ckt,
    cv,
    cs,
    sc,
    best,
    top,
    acc,
    *,
    chunk,
    c,
):
    sources = got_ref.shape[0]
    cents = 2 * sources
    width = out_ref.shape[1] - 16
    block = sc.shape[0]

    tails = got_ref[:, 2 * PAGE : ROWS, :].astype(jnp.float32).reshape(sources * TAIL, HEAD)
    tails = tails.astype(jnp.bfloat16)
    r = lax.broadcasted_iota(jnp.int32, (cents, sources * TAIL), 0)
    col = lax.broadcasted_iota(jnp.int32, (cents, sources * TAIL), 1)
    first = (r // 2) * TAIL + r % 2
    cents_of = [
        jnp.dot(
            (col == first + off).astype(jnp.float32).astype(jnp.bfloat16),
            tails,
            preferred_element_type=jnp.float32,
        )
        for off in (0, 2)
    ]
    ckt[...] = jnp.transpose(cents_of[0]).astype(jnp.bfloat16)
    cv[:, :HEAD] = cents_of[1].astype(jnp.bfloat16)
    cv[:, HEAD:] = jnp.ones((cents, HEAD), jnp.bfloat16)

    def place(s, at):
        rows = pl.ds(at, PAGE)
        keys[rows, :] = got_ref[s, 0:PAGE, :].astype(jnp.float32)
        values[rows, :] = got_ref[s, PAGE : 2 * PAGE, :].astype(jnp.float32)
        return at + live_ref[s]

    end = lax.fori_loop(0, sources, place, 0, unroll=4)
    half = chunk // 2
    halves = (end + half - 1) // half
    chunks = halves // 2
    rest = pl.ds(end, chunk)
    keys[rest, :] = jnp.broadcast_to(keys[0:1, :], (chunk, HEAD))
    values[rest, :] = jnp.zeros((chunk, HEAD), jnp.float32)
    number = lax.broadcasted_iota(jnp.int32, (HEAD, HEAD), 0)

    def turn(j, carry):
        for k in range(0, chunk, HEAD):
            start = pl.multiple_of(j * chunk + k, HEAD)
            at = pl.ds(start, HEAD)
            kt[:, at] = jnp.transpose(keys[at, :]).astype(jnp.bfloat16)
            vv[at, :HEAD] = values[at, :].astype(jnp.bfloat16)
            vv[at, HEAD:] = jnp.where(number + start < end, 1.0, 0.0).astype(jnp.bfloat16)
        return carry

    lax.fori_loop(0, (halves + 1) // 2, turn, 0)

    def each_chunk(body):
        def whole(j, carry):
            body(pl.ds(pl.multiple_of(j * chunk, chunk), chunk))
            return carry

        lax.fori_loop(0, chunks, whole, 0)

        @pl.when(halves % 2 == 1)
        def _():
            body(pl.ds(pl.multiple_of(chunks * chunk, chunk), half))

    for first in range(0, q_ref.shape[0], block):
        score = jnp.dot(q_ref[first : first + block, :], ckt[...], preferred_element_type=jnp.float32) + cbias_ref[...]
        cs[...] = score
        best[...] = score

        def scores(at, first=first):
            score = jnp.dot(
                q_ref[first : first + block, :], kt[:, at], preferred_element_type=jnp.float32
            )
            sc[:, at] = score
            parts = [score[:, k : k + HEAD] for k in range(0, at.size, HEAD)]
            best[...] = jnp.maximum(best[...], functools.reduce(jnp.maximum, parts))

        each_chunk(scores)
        top[...] = jnp.broadcast_to(jnp.max(best[...], axis=1, keepdims=True), (block, HEAD))
        weight = jnp.exp((cs[...] - top[...]) * c).astype(jnp.bfloat16)
        acc[...] = jnp.dot(weight, cv[...], preferred_element_type=jnp.float32)

        def weighted(at):
            tops = jnp.concatenate([top[...]] * (at.size // HEAD), axis=1)
            weight = jnp.exp((sc[:, at] - tops) * c).astype(jnp.bfloat16)
            acc[...] += jnp.dot(weight, vv[at, :], preferred_element_type=jnp.float32)

        each_chunk(weighted)
        lanes = lax.broadcasted_iota(jnp.int32, (width, HEAD), 1)
        row = lax.broadcasted_iota(jnp.int32, (16, HEAD), 0)
        for z in range(block // width):
            at = slice(z * width, (z + 1) * width)
            to = RING.index(first // width + z)
            total = acc[at, HEAD:]
            out_ref[to, :width, :] = (acc[at, :HEAD] / total).astype(jnp.bfloat16)
            stats = jnp.transpose(jnp.where(lanes == 0, top[at, :], total))
            tile = jnp.zeros((16, HEAD), jnp.float32)
            for i, piece in enumerate(split3(stats[0:1, :]) + split3(stats[1:2, :])):
                for h in range(2):
                    tile = jnp.where(row == 2 * i + h, piece[:, h * HEAD : (h + 1) * HEAD], tile)
            out_ref[to, width:, :] = tile.astype(jnp.bfloat16)


def attend(live, cbias, got, rows, parts, c):
    sources = got.shape[0]
    chunk = 512
    block = rows.shape[0] // 2
    slots = sources * PAGE
    cents = 2 * sources
    width = rows.shape[0] // parts
    vmem = pl.BlockSpec(memory_space=pltpu.VMEM)
    return pl.pallas_call(
        functools.partial(attend_kernel, chunk=chunk, c=c),
        in_specs=[pl.BlockSpec(memory_space=pltpu.SMEM), vmem, vmem, vmem],
        out_specs=vmem,
        scratch_shapes=[
            pltpu.VMEM((slots + chunk, HEAD), jnp.float32),
            pltpu.VMEM((slots + chunk, HEAD), jnp.float32),
            pltpu.VMEM((HEAD, slots), jnp.bfloat16),
            pltpu.VMEM((slots, 2 * HEAD), jnp.bfloat16),
            pltpu.VMEM((HEAD, cents), jnp.bfloat16),
            pltpu.VMEM((cents, 2 * HEAD), jnp.bfloat16),
            pltpu.VMEM((block, cents), jnp.float32),
            pltpu.VMEM((block, slots), jnp.float32),
            pltpu.VMEM((block, HEAD), jnp.float32),
            pltpu.VMEM((block, HEAD), jnp.float32),
            pltpu.VMEM((block, 2 * HEAD), jnp.float32),
        ],
        out_shape=jax.ShapeDtypeStruct((parts, width + 16, HEAD), jnp.bfloat16),
        compiler_params=pltpu.CompilerParams(vmem_limit_bytes=40 * MiB),
        cost_estimate=pl.CostEstimate(
            flops=4 * rows.shape[0] * (slots + cents) * HEAD,
            bytes_accessed=4 * MiB,
            transcendentals=rows.shape[0] * (slots + cents),
        ),
        name="attend",
    )(live, cbias, got, rows)


def merge_kernel(got_ref, out_ref, *, c):
    parts = got_ref.shape[0]
    block = out_ref.shape[1]
    tops, totals = [], []
    for z in range(parts):
        tile = got_ref[z, block:, :].astype(jnp.float32)
        tops.append(tile[0:2] + tile[2:4] + tile[4:6])
        totals.append(tile[6:8] + tile[8:10] + tile[10:12])
    top = functools.reduce(jnp.maximum, tops)
    factors = [t * jnp.exp((m - top) * c) for m, t in zip(tops, totals)]
    whole = functools.reduce(jnp.add, factors)
    columns = jnp.transpose(jnp.concatenate([f / whole for f in factors], axis=0))
    for h in range(2):
        at = slice(h * HEAD, (h + 1) * HEAD)
        out = jnp.zeros((HEAD, HEAD), jnp.float32)
        for z in range(parts):
            column = columns[:, 2 * z + h : 2 * z + h + 1]
            out += got_ref[z, at, :].astype(jnp.float32) * column
        out = out.astype(jnp.bfloat16)
        for z in range(parts):
            out_ref[z, at, :] = out


def merge(got, c):
    parts, block, unused = got.shape
    block -= 16
    return pl.pallas_call(
        functools.partial(merge_kernel, c=c),
        out_shape=jax.ShapeDtypeStruct((parts, block, HEAD), jnp.bfloat16),
        compiler_params=pltpu.CompilerParams(vmem_limit_bytes=16 * MiB),
        name="merge",
    )(got)


def exchange(blocks, axis, order):
    return lax.all_to_all(
        blocks, axis, split_axis=0, concat_axis=0, axis_index_groups=[order], tiled=True
    )


def local(cache_keys, cache_values, counts, listed, queries):
    ctx_n = lax.axis_size("ctx")
    split_n = lax.axis_size("split")
    items, pages_here, page_len, head = cache_keys.shape
    requests = counts.shape[0]
    kv_heads = items // requests
    root = head**0.5
    c = head**-0.5
    item = lax.axis_index("ctx")
    split_idx = lax.axis_index("split")
    first = (item * split_n + split_idx) * pages_here
    message = pack(first.reshape(1), counts, listed, cache_keys, cache_values)
    got = exchange(message, "ctx", CTX)

    sel_row = lax.dynamic_index_in_dim(listed, item, 0, keepdims=False)
    count_row = lax.dynamic_index_in_dim(counts, item // kv_heads, 0, keepdims=False)
    mine = count_row.reshape(ctx_n, split_n, pages_here)
    mine = lax.dynamic_index_in_dim(mine, split_idx, 1, keepdims=False)
    mine = mine.reshape(4, 8, 2, pages_here).transpose(2, 0, 1, 3)
    mine = jnp.stack([mine[:, :, y] for y in RING], axis=2).reshape(ctx_n, pages_here)
    source = jnp.array(CTX, jnp.int32)[:, None]
    candidate = (source * split_n + split_idx) * pages_here + jnp.arange(
        pages_here, dtype=jnp.int32
    )
    marks = jnp.any(sel_row[None, None, :] == candidate[:, :, None], axis=2)
    live = jnp.sum(jnp.where(marks, mine, 0), axis=1)
    cbias = jnp.where(marks, NEG, jnp.log(mine.astype(jnp.float32)) * root)
    rows = queries.reshape(-1, head)
    partial = attend(live, cbias.reshape(1, -1), got, rows, split_n, c)
    shared = exchange(partial, "split", RING)
    out = exchange(merge(shared, c), "split", RING)
    out = jnp.concatenate([out[RING.index(z)] for z in range(split_n)], axis=0)
    return out.astype(jnp.float32).reshape(queries.shape)


def solution(mesh):
    return jax.shard_map(
        local,
        mesh=mesh,
        in_specs=(
            P(None, ("ctx", "split"), None, None),
            P(None, ("ctx", "split"), None, None),
            P(),
            P(),
            P("ctx", None, None, None),
        ),
        out_specs=P("ctx", None, None, None),
        check_vma=False,
    )
```

```python
import functools

import jax
import jax.numpy as jnp
from jax import lax
from jax.experimental import pallas as pl
from jax.experimental.pallas import tpu as pltpu
from jax.sharding import PartitionSpec as P

NEG = -1e30

PAGE = 64
HEAD = 128
TAIL = 8
ROWS = 2 * PAGE + TAIL
MiB = 1024 * 1024

RING = [3 * i % 8 for i in range(8)]
CTX = [(x * 8 + y) * 2 + core for core in range(2) for x in range(4) for y in RING]


def pack_kernel(
    page_ref,
    counts_ref,
    listed_ref,
    keys_ref,
    values_ref,
    out_ref,
    cache,
    message,
    count_here,
    listed,
    got,
    sent,
    small,
):
    items = out_ref.shape[0]
    page = page_ref[0]
    kv_heads = 4
    block = 4
    groups = items // block

    def fetch(g):
        at = pl.ds(g * block, block)
        return [
            pltpu.make_async_copy(ref.at[at], cache.at[at, a], got.at[a, g])
            for a, ref in enumerate((keys_ref, values_ref))
        ]

    def send(item):
        to = CTX.index(item)
        return pltpu.make_async_copy(message.at[to], out_ref.at[to], sent.at[item])

    columns = pl.ds(pl.multiple_of((page // HEAD) * HEAD, HEAD), HEAD)
    lists = pltpu.make_async_copy(listed_ref, listed, small.at[0])
    numbers = pltpu.make_async_copy(counts_ref.at[:, columns], count_here, small.at[1])
    lists.start()
    numbers.start()
    for g in range(groups):
        for a, copy in enumerate(fetch(g)):
            copy.start(priority=a)
    lists.wait()
    second = jnp.max(jnp.where(listed[...] == page + 1, 1.0, 0.0), axis=1, keepdims=True)
    numbers.wait()
    row = lax.broadcasted_iota(jnp.int32, (16, 4 * PAGE), 0)
    slot = lax.broadcasted_iota(jnp.int32, (16, 4 * PAGE), 1)
    quarter = slot // PAGE
    slot = slot % PAGE
    out_row = lax.broadcasted_iota(jnp.int32, (16, HEAD), 0)
    for g in range(groups):
        for copy in fetch(g):
            copy.wait()
        for item in range(g * block, (g + 1) * block):
            to = CTX.index(item)
            choice = jnp.broadcast_to(second[item : item + 1, :], (PAGE, HEAD)) > 0.5
            for a in range(2):
                message[to, a * PAGE : (a + 1) * PAGE, :] = jnp.where(
                    choice, cache[item, a, 1], cache[item, a, 0]
                )
        for item in range(g * block, (g + 1) * block, 2):
            if item % kv_heads == 0:
                request = item // kv_heads
                count = [count_here[request, page % HEAD + p] for p in range(2)]
                limit = jnp.where(row % 2 == 0, count[0], count[1])
                live = jnp.logical_and(quarter == row, slot < limit)
                live = jnp.where(live, 1.0, 0.0).astype(jnp.bfloat16)
                divisor = jnp.where(out_row % 2 == 0, count[0], count[1]).astype(jnp.float32)
                inverse = 1.0 / divisor
            both = jnp.concatenate(
                [cache[i].reshape(4 * PAGE, HEAD) for i in (item, item + 1)], axis=1
            )
            total = jnp.dot(live, both, preferred_element_type=jnp.float32)
            for k in range(2):
                mean = total[:, k * HEAD : (k + 1) * HEAD] * inverse
                message[CTX.index(item + k), 2 * PAGE : ROWS, :] = mean[:TAIL].astype(jnp.bfloat16)
            for i in (item, item + 1):
                send(i).start(priority=i % 2)
    for item in range(items):
        send(item).wait()


def pack(page, counts, listed, cache_keys, cache_values):
    items = cache_keys.shape[0]
    groups = items // 4
    whole = pl.BlockSpec(memory_space=pl.ANY)
    return pl.pallas_call(
        pack_kernel,
        in_specs=[pl.BlockSpec(memory_space=pltpu.SMEM), whole, whole, whole, whole],
        out_specs=whole,
        out_shape=jax.ShapeDtypeStruct((items, ROWS, HEAD), jnp.bfloat16),
        scratch_shapes=[
            pltpu.VMEM((items, 2, 2, PAGE, HEAD), jnp.bfloat16),
            pltpu.VMEM((items, ROWS, HEAD), jnp.bfloat16),
            pltpu.SMEM((counts.shape[0], HEAD), jnp.int32),
            pltpu.VMEM(listed.shape, jnp.int32),
            pltpu.SemaphoreType.DMA((2, groups)),
            pltpu.SemaphoreType.DMA((items,)),
            pltpu.SemaphoreType.DMA((2,)),
        ],
        compiler_params=pltpu.CompilerParams(vmem_limit_bytes=58 * MiB),
        name="pack",
    )(page, counts, listed, cache_keys, cache_values)


def split3(x):
    high = x.astype(jnp.bfloat16).astype(jnp.float32)
    rest = x - high
    middle = rest.astype(jnp.bfloat16).astype(jnp.float32)
    return high, middle, rest - middle


def attend_kernel(
    live_ref,
    cbias_ref,
    got_ref,
    q_ref,
    out_ref,
    keys,
    values,
    kb,
    vv,
    ckt,
    cv,
    cs,
    sc,
    best,
    top,
    acc,
    *,
    chunk,
    c,
):
    sources = got_ref.shape[0]
    cents = 2 * sources
    width = out_ref.shape[1] - TAIL
    block = sc.shape[0]

    tails = got_ref[:, 2 * PAGE : ROWS, :].astype(jnp.float32).reshape(sources * TAIL, HEAD)
    tails = tails.astype(jnp.bfloat16)
    r = lax.broadcasted_iota(jnp.int32, (cents, sources * TAIL), 0)
    col = lax.broadcasted_iota(jnp.int32, (cents, sources * TAIL), 1)
    first = (r // 2) * TAIL + r % 2
    cents_of = [
        jnp.dot(
            (col == first + off).astype(jnp.float32).astype(jnp.bfloat16),
            tails,
            preferred_element_type=jnp.float32,
        )
        for off in (0, 2)
    ]
    ckt[...] = jnp.transpose(cents_of[0]).astype(jnp.bfloat16)
    cv[:, :HEAD] = cents_of[1].astype(jnp.bfloat16)
    cv[:, HEAD:] = jnp.ones((cents, HEAD), jnp.bfloat16)

    def place(s, at):
        rows = pl.ds(at, PAGE)
        keys[rows, :] = got_ref[s, 0:PAGE, :].astype(jnp.float32)
        values[rows, :] = got_ref[s, PAGE : 2 * PAGE, :].astype(jnp.float32)
        return at + live_ref[s]

    end = lax.fori_loop(0, sources, place, 0, unroll=4)
    half = chunk // 2
    halves = (end + half - 1) // half
    chunks = halves // 2
    rest = pl.ds(end, chunk)
    keys[rest, :] = jnp.broadcast_to(keys[0:1, :], (chunk, HEAD))
    values[rest, :] = jnp.zeros((chunk, HEAD), jnp.float32)
    number = lax.broadcasted_iota(jnp.int32, (HEAD, HEAD), 0)

    def turn(j, carry):
        for k in range(0, chunk, HEAD):
            start = pl.multiple_of(j * chunk + k, HEAD)
            at = pl.ds(start, HEAD)
            kb[at, :] = keys[at, :].astype(jnp.bfloat16)
            vv[at, :HEAD] = values[at, :].astype(jnp.bfloat16)
            vv[at, HEAD:] = jnp.where(number + start < end, 1.0, 0.0).astype(jnp.bfloat16)
        return carry

    lax.fori_loop(0, (halves + 1) // 2, turn, 0)

    def each_chunk(body):
        def whole(j, carry):
            body(pl.ds(pl.multiple_of(j * chunk, chunk), chunk))
            return carry

        lax.fori_loop(0, chunks, whole, 0)

        @pl.when(halves % 2 == 1)
        def _():
            body(pl.ds(pl.multiple_of(chunks * chunk, chunk), half))

    for first in range(0, q_ref.shape[0], block):
        score = jnp.dot(q_ref[first : first + block, :], ckt[...], preferred_element_type=jnp.float32) + cbias_ref[...]
        cs[...] = score
        best[...] = score

        def scores(at, first=first):
            score = lax.dot_general(
                q_ref[first : first + block, :],
                kb[at, :],
                (((1,), (1,)), ((), ())),
                preferred_element_type=jnp.float32,
            )
            sc[:, at] = score
            parts = [score[:, k : k + HEAD] for k in range(0, at.size, HEAD)]
            best[...] = jnp.maximum(best[...], functools.reduce(jnp.maximum, parts))

        each_chunk(scores)
        top[...] = jnp.broadcast_to(jnp.max(best[...], axis=1, keepdims=True), (block, HEAD))
        weight = jnp.exp((cs[...] - top[...]) * c).astype(jnp.bfloat16)
        acc[...] = jnp.dot(weight, cv[...], preferred_element_type=jnp.float32)

        def weighted(at):
            tops = jnp.concatenate([top[...]] * (at.size // HEAD), axis=1)
            weight = jnp.exp((sc[:, at] - tops) * c).astype(jnp.bfloat16)
            acc[...] += jnp.dot(weight, vv[at, :], preferred_element_type=jnp.float32)

        each_chunk(weighted)
        row = lax.broadcasted_iota(jnp.int32, (TAIL, HEAD), 0)
        for z in range(block // width):
            at = slice(z * width, (z + 1) * width)
            to = RING.index(first // width + z)
            total = acc[at, HEAD:]
            out_ref[to, :width, :] = (acc[at, :HEAD] / total).astype(jnp.bfloat16)
            stats = jnp.transpose(top[at, :] + jnp.log(total) * (1.0 / c))
            tile = jnp.zeros((TAIL, HEAD), jnp.float32)
            for i, piece in enumerate(split3(stats[0:1, :])):
                for h in range(2):
                    tile = jnp.where(row == 2 * i + h, piece[:, h * HEAD : (h + 1) * HEAD], tile)
            out_ref[to, width:, :] = tile.astype(jnp.bfloat16)


def attend(live, cbias, got, rows, parts, c):
    sources = got.shape[0]
    chunk = 512
    block = rows.shape[0] // 2
    slots = sources * PAGE
    cents = 2 * sources
    width = rows.shape[0] // parts
    vmem = pl.BlockSpec(memory_space=pltpu.VMEM)
    return pl.pallas_call(
        functools.partial(attend_kernel, chunk=chunk, c=c),
        in_specs=[pl.BlockSpec(memory_space=pltpu.SMEM), vmem, vmem, vmem],
        out_specs=vmem,
        scratch_shapes=[
            pltpu.VMEM((slots + chunk, HEAD), jnp.float32),
            pltpu.VMEM((slots + chunk, HEAD), jnp.float32),
            pltpu.VMEM((slots, HEAD), jnp.bfloat16),
            pltpu.VMEM((slots, 2 * HEAD), jnp.bfloat16),
            pltpu.VMEM((HEAD, cents), jnp.bfloat16),
            pltpu.VMEM((cents, 2 * HEAD), jnp.bfloat16),
            pltpu.VMEM((block, cents), jnp.float32),
            pltpu.VMEM((block, slots), jnp.float32),
            pltpu.VMEM((block, HEAD), jnp.float32),
            pltpu.VMEM((block, HEAD), jnp.float32),
            pltpu.VMEM((block, 2 * HEAD), jnp.float32),
        ],
        out_shape=jax.ShapeDtypeStruct((parts, width + TAIL, HEAD), jnp.bfloat16),
        compiler_params=pltpu.CompilerParams(vmem_limit_bytes=40 * MiB),
        cost_estimate=pl.CostEstimate(
            flops=4 * rows.shape[0] * (slots + cents) * HEAD,
            bytes_accessed=4 * MiB,
            transcendentals=rows.shape[0] * (slots + cents),
        ),
        name="attend",
    )(live, cbias, got, rows)


def merge_kernel(got_ref, out_ref, *, c):
    parts = got_ref.shape[0]
    block = out_ref.shape[1]
    sums = []
    for z in range(parts):
        tile = got_ref[z, block:, :].astype(jnp.float32)
        sums.append(tile[0:2] + tile[2:4] + tile[4:6])
    top = functools.reduce(jnp.maximum, sums)
    factors = [jnp.exp((m - top) * c) for m in sums]
    whole = functools.reduce(jnp.add, factors)
    columns = jnp.transpose(jnp.concatenate([f / whole for f in factors], axis=0))
    for h in range(2):
        at = slice(h * HEAD, (h + 1) * HEAD)
        out = jnp.zeros((HEAD, HEAD), jnp.float32)
        for z in range(parts):
            column = columns[:, 2 * z + h : 2 * z + h + 1]
            out += got_ref[z, at, :].astype(jnp.float32) * column
        out = out.astype(jnp.bfloat16)
        for z in range(parts):
            out_ref[z, at, :] = out


def merge(got, c):
    parts, block, unused = got.shape
    block -= TAIL
    return pl.pallas_call(
        functools.partial(merge_kernel, c=c),
        out_shape=jax.ShapeDtypeStruct((parts, block, HEAD), jnp.bfloat16),
        compiler_params=pltpu.CompilerParams(vmem_limit_bytes=16 * MiB),
        name="merge",
    )(got)


def exchange(blocks, axis, order):
    return lax.all_to_all(
        blocks, axis, split_axis=0, concat_axis=0, axis_index_groups=[order], tiled=True
    )


def local(cache_keys, cache_values, counts, listed, queries):
    ctx_n = lax.axis_size("ctx")
    split_n = lax.axis_size("split")
    items, pages_here, page_len, head = cache_keys.shape
    requests = counts.shape[0]
    kv_heads = items // requests
    root = head**0.5
    c = head**-0.5
    item = lax.axis_index("ctx")
    split_idx = lax.axis_index("split")
    first = (item * split_n + split_idx) * pages_here
    message = pack(first.reshape(1), counts, listed, cache_keys, cache_values)
    got = exchange(message, "ctx", CTX)

    sel_row = lax.dynamic_index_in_dim(listed, item, 0, keepdims=False)
    count_row = lax.dynamic_index_in_dim(counts, item // kv_heads, 0, keepdims=False)
    mine = count_row.reshape(ctx_n, split_n, pages_here)
    mine = lax.dynamic_index_in_dim(mine, split_idx, 1, keepdims=False)
    mine = mine.reshape(4, 8, 2, pages_here).transpose(2, 0, 1, 3)
    mine = jnp.stack([mine[:, :, y] for y in RING], axis=2).reshape(ctx_n, pages_here)
    source = jnp.array(CTX, jnp.int32)[:, None]
    candidate = (source * split_n + split_idx) * pages_here + jnp.arange(
        pages_here, dtype=jnp.int32
    )
    marks = jnp.any(sel_row[None, None, :] == candidate[:, :, None], axis=2)
    live = jnp.sum(jnp.where(marks, mine, 0), axis=1)
    cbias = jnp.where(marks, NEG, jnp.log(mine.astype(jnp.float32)) * root)
    rows = queries.reshape(-1, head)
    partial = attend(live, cbias.reshape(1, -1), got, rows, split_n, c)
    shared = exchange(partial, "split", RING)
    out = exchange(merge(shared, c), "split", RING)
    out = jnp.concatenate([out[RING.index(z)] for z in range(split_n)], axis=0)
    return out.astype(jnp.float32).reshape(queries.shape)


def solution(mesh):
    return jax.shard_map(
        local,
        mesh=mesh,
        in_specs=(
            P(None, ("ctx", "split"), None, None),
            P(None, ("ctx", "split"), None, None),
            P(),
            P(),
            P("ctx", None, None, None),
        ),
        out_specs=P("ctx", None, None, None),
        check_vma=False,
    )
```

```python
import functools

import jax
import jax.numpy as jnp
from jax import lax
from jax.experimental import pallas as pl
from jax.experimental.pallas import tpu as pltpu
from jax.sharding import PartitionSpec as P

NEG = -1e30

PAGE = 64
HEAD = 128
TAIL = 8
ROWS = 2 * PAGE + TAIL
MiB = 1024 * 1024

RING = [3 * i % 8 for i in range(8)]
CTX = [(x * 8 + y) * 2 + core for core in range(2) for x in range(4) for y in RING]


GROUPS = [(0, 24), (24, 24), (48, 16)]
SENDS = [(at, 8) for at in range(0, 64, 8) if CTX[at] < 48]
SENDS += [(at, 1) for at in range(64) if CTX[at] >= 48]


def pack_kernel(
    page_ref,
    counts_ref,
    listed_ref,
    keys_ref,
    values_ref,
    out_ref,
    cache,
    message,
    count_here,
    listed,
    got,
    sent,
    small,
):
    items = out_ref.shape[0]
    page = page_ref[0]
    kv_heads = 4

    def fetch(g):
        at = pl.ds(GROUPS[g][0], GROUPS[g][1])
        return [
            pltpu.make_async_copy(ref.at[at], cache.at[a, at], got.at[a, g])
            for a, ref in enumerate((keys_ref, values_ref))
        ]

    def send(k):
        at = pl.ds(SENDS[k][0], SENDS[k][1])
        return pltpu.make_async_copy(message.at[at], out_ref.at[at], sent.at[k])

    columns = pl.ds(pl.multiple_of((page // HEAD) * HEAD, HEAD), HEAD)
    lists = pltpu.make_async_copy(listed_ref, listed, small.at[0])
    numbers = pltpu.make_async_copy(counts_ref.at[:, columns], count_here, small.at[1])
    lists.start()
    numbers.start()
    for g in range(len(GROUPS)):
        for a, copy in enumerate(fetch(g)):
            copy.start(priority=a)
    lists.wait()
    second = jnp.max(jnp.where(listed[...] == page + 1, 1.0, 0.0), axis=1, keepdims=True)
    numbers.wait()
    row = lax.broadcasted_iota(jnp.int32, (16, 4 * PAGE), 0)
    slot = lax.broadcasted_iota(jnp.int32, (16, 4 * PAGE), 1)
    quarter = slot // PAGE
    slot = slot % PAGE
    out_row = lax.broadcasted_iota(jnp.int32, (16, HEAD), 0)
    ready = set()
    for g, (first, number) in enumerate(GROUPS):
        for copy in fetch(g):
            copy.wait()
        for item in range(first, first + number):
            to = CTX.index(item)
            choice = jnp.broadcast_to(second[item : item + 1, :], (PAGE, HEAD)) > 0.5
            for a in range(2):
                message[to, a * PAGE : (a + 1) * PAGE, :] = jnp.where(
                    choice, cache[a, item, 1], cache[a, item, 0]
                )
        for item in range(first, first + number, 2):
            if item % kv_heads == 0:
                request = item // kv_heads
                count = [count_here[request, page % HEAD + p] for p in range(2)]
                limit = jnp.where(row % 2 == 0, count[0], count[1])
                live = jnp.logical_and(quarter == row, slot < limit)
                live = jnp.where(live, 1.0, 0.0).astype(jnp.bfloat16)
                divisor = jnp.where(out_row % 2 == 0, count[0], count[1]).astype(jnp.float32)
                inverse = 1.0 / divisor
            both = jnp.concatenate(
                [
                    jnp.concatenate([cache[a, i].reshape(2 * PAGE, HEAD) for a in range(2)], axis=0)
                    for i in (item, item + 1)
                ],
                axis=1,
            )
            total = jnp.dot(live, both, preferred_element_type=jnp.float32)
            for k in range(2):
                mean = total[:, k * HEAD : (k + 1) * HEAD] * inverse
                message[CTX.index(item + k), 2 * PAGE : ROWS, :] = mean[:TAIL].astype(jnp.bfloat16)
            ready.update((CTX.index(item), CTX.index(item + 1)))
            for k, (at, size) in enumerate(SENDS):
                if ready.issuperset(range(at, at + size)):
                    send(k).start(priority=k % 2)
                    ready.difference_update(range(at, at + size))
    for k in range(len(SENDS)):
        send(k).wait()


def pack(page, counts, listed, cache_keys, cache_values):
    items = cache_keys.shape[0]
    whole = pl.BlockSpec(memory_space=pl.ANY)
    return pl.pallas_call(
        pack_kernel,
        in_specs=[pl.BlockSpec(memory_space=pltpu.SMEM), whole, whole, whole, whole],
        out_specs=whole,
        out_shape=jax.ShapeDtypeStruct((items, ROWS, HEAD), jnp.bfloat16),
        scratch_shapes=[
            pltpu.VMEM((2, items, 2, PAGE, HEAD), jnp.bfloat16),
            pltpu.VMEM((items, ROWS, HEAD), jnp.bfloat16),
            pltpu.SMEM((counts.shape[0], HEAD), jnp.int32),
            pltpu.VMEM(listed.shape, jnp.int32),
            pltpu.SemaphoreType.DMA((2, len(GROUPS))),
            pltpu.SemaphoreType.DMA((len(SENDS),)),
            pltpu.SemaphoreType.DMA((2,)),
        ],
        compiler_params=pltpu.CompilerParams(vmem_limit_bytes=58 * MiB),
        name="pack",
    )(page, counts, listed, cache_keys, cache_values)


def split3(x):
    high = x.astype(jnp.bfloat16).astype(jnp.float32)
    rest = x - high
    middle = rest.astype(jnp.bfloat16).astype(jnp.float32)
    return high, middle, rest - middle


def attend_kernel(
    live_ref,
    cbias_ref,
    got_ref,
    q_ref,
    out_ref,
    keys,
    values,
    kt,
    vv,
    ckt,
    cv,
    cs,
    sc,
    best,
    top,
    acc,
    *,
    chunk,
    c,
):
    sources = got_ref.shape[0]
    cents = 2 * sources
    width = out_ref.shape[1] - TAIL
    block = sc.shape[0]

    tails = got_ref[:, 2 * PAGE : ROWS, :].astype(jnp.float32).reshape(sources * TAIL, HEAD)
    tails = tails.astype(jnp.bfloat16)
    r = lax.broadcasted_iota(jnp.int32, (cents, sources * TAIL), 0)
    col = lax.broadcasted_iota(jnp.int32, (cents, sources * TAIL), 1)
    first = (r // 2) * TAIL + r % 2
    cents_of = [
        jnp.dot(
            (col == first + off).astype(jnp.float32).astype(jnp.bfloat16),
            tails,
            preferred_element_type=jnp.float32,
        )
        for off in (0, 2)
    ]
    ckt[...] = jnp.transpose(cents_of[0]).astype(jnp.bfloat16)
    cv[:, :HEAD] = cents_of[1].astype(jnp.bfloat16)
    cv[:, HEAD:] = jnp.ones((cents, HEAD), jnp.bfloat16)

    def place(s, at):
        rows = pl.ds(at, PAGE)
        keys[rows, :] = got_ref[s, 0:PAGE, :].astype(jnp.float32)
        values[rows, :] = got_ref[s, PAGE : 2 * PAGE, :].astype(jnp.float32)
        return at + live_ref[s]

    end = lax.fori_loop(0, sources, place, 0, unroll=4)
    half = chunk // 2
    halves = (end + half - 1) // half
    chunks = halves // 2
    rest = pl.ds(end, chunk)
    keys[rest, :] = jnp.broadcast_to(keys[0:1, :], (chunk, HEAD))
    values[rest, :] = jnp.zeros((chunk, HEAD), jnp.float32)
    number = lax.broadcasted_iota(jnp.int32, (HEAD, HEAD), 0)

    def turn(j, carry):
        for k in range(0, chunk, HEAD):
            start = pl.multiple_of(j * chunk + k, HEAD)
            at = pl.ds(start, HEAD)
            kt[:, at] = jnp.transpose(keys[at, :]).astype(jnp.bfloat16)
            vv[at, :HEAD] = values[at, :].astype(jnp.bfloat16)
            vv[at, HEAD:] = jnp.where(number + start < end, 1.0, 0.0).astype(jnp.bfloat16)
        return carry

    lax.fori_loop(0, (halves + 1) // 2, turn, 0)

    def each_chunk(body):
        def whole(j, carry):
            body(pl.ds(pl.multiple_of(j * chunk, chunk), chunk))
            return carry

        lax.fori_loop(0, chunks, whole, 0)

        @pl.when(halves % 2 == 1)
        def _():
            body(pl.ds(pl.multiple_of(chunks * chunk, chunk), half))

    for first in range(0, q_ref.shape[0], block):
        score = jnp.dot(q_ref[first : first + block, :], ckt[...], preferred_element_type=jnp.float32) + cbias_ref[...]
        cs[...] = score
        best[...] = score

        def scores(at, first=first):
            score = jnp.dot(
                q_ref[first : first + block, :], kt[:, at], preferred_element_type=jnp.float32
            )
            sc[:, at] = score
            parts = [score[:, k : k + HEAD] for k in range(0, at.size, HEAD)]
            best[...] = jnp.maximum(best[...], functools.reduce(jnp.maximum, parts))

        each_chunk(scores)
        top[...] = jnp.broadcast_to(jnp.max(best[...], axis=1, keepdims=True), (block, HEAD))
        weight = jnp.exp((cs[...] - top[...]) * c).astype(jnp.bfloat16)
        acc[...] = jnp.dot(weight, cv[...], preferred_element_type=jnp.float32)

        def weighted(at):
            tops = jnp.concatenate([top[...]] * (at.size // HEAD), axis=1)
            weight = jnp.exp((sc[:, at] - tops) * c).astype(jnp.bfloat16)
            acc[...] += jnp.dot(weight, vv[at, :], preferred_element_type=jnp.float32)

        each_chunk(weighted)
        row = lax.broadcasted_iota(jnp.int32, (TAIL, HEAD), 0)
        for z in range(block // width):
            at = slice(z * width, (z + 1) * width)
            to = RING.index(first // width + z)
            total = acc[at, HEAD:]
            out_ref[to, :width, :] = (acc[at, :HEAD] / total).astype(jnp.bfloat16)
            stats = jnp.transpose(top[at, :] + jnp.log(total) * (1.0 / c))
            tile = jnp.zeros((TAIL, HEAD), jnp.float32)
            for i, piece in enumerate(split3(stats[0:1, :])):
                for h in range(2):
                    tile = jnp.where(row == 2 * i + h, piece[:, h * HEAD : (h + 1) * HEAD], tile)
            out_ref[to, width:, :] = tile.astype(jnp.bfloat16)


def attend(live, cbias, got, rows, parts, c):
    sources = got.shape[0]
    chunk = 512
    block = rows.shape[0] // 2
    slots = sources * PAGE
    cents = 2 * sources
    width = rows.shape[0] // parts
    vmem = pl.BlockSpec(memory_space=pltpu.VMEM)
    return pl.pallas_call(
        functools.partial(attend_kernel, chunk=chunk, c=c),
        in_specs=[pl.BlockSpec(memory_space=pltpu.SMEM), vmem, vmem, vmem],
        out_specs=vmem,
        scratch_shapes=[
            pltpu.VMEM((slots + chunk, HEAD), jnp.float32),
            pltpu.VMEM((slots + chunk, HEAD), jnp.float32),
            pltpu.VMEM((HEAD, slots), jnp.bfloat16),
            pltpu.VMEM((slots, 2 * HEAD), jnp.bfloat16),
            pltpu.VMEM((HEAD, cents), jnp.bfloat16),
            pltpu.VMEM((cents, 2 * HEAD), jnp.bfloat16),
            pltpu.VMEM((block, cents), jnp.float32),
            pltpu.VMEM((block, slots), jnp.float32),
            pltpu.VMEM((block, HEAD), jnp.float32),
            pltpu.VMEM((block, HEAD), jnp.float32),
            pltpu.VMEM((block, 2 * HEAD), jnp.float32),
        ],
        out_shape=jax.ShapeDtypeStruct((parts, width + TAIL, HEAD), jnp.bfloat16),
        compiler_params=pltpu.CompilerParams(vmem_limit_bytes=40 * MiB),
        cost_estimate=pl.CostEstimate(
            flops=4 * rows.shape[0] * (slots + cents) * HEAD,
            bytes_accessed=4 * MiB,
            transcendentals=rows.shape[0] * (slots + cents),
        ),
        name="attend",
    )(live, cbias, got, rows)


def merge_kernel(got_ref, out_ref, *, c):
    parts = got_ref.shape[0]
    block = out_ref.shape[1]
    sums = []
    for z in range(parts):
        tile = got_ref[z, block:, :].astype(jnp.float32)
        sums.append(tile[0:2] + tile[2:4] + tile[4:6])
    top = functools.reduce(jnp.maximum, sums)
    factors = [jnp.exp((m - top) * c) for m in sums]
    whole = functools.reduce(jnp.add, factors)
    columns = jnp.transpose(jnp.concatenate([f / whole for f in factors], axis=0))
    for h in range(2):
        at = slice(h * HEAD, (h + 1) * HEAD)
        out = jnp.zeros((HEAD, HEAD), jnp.float32)
        for z in range(parts):
            column = columns[:, 2 * z + h : 2 * z + h + 1]
            out += got_ref[z, at, :].astype(jnp.float32) * column
        out = out.astype(jnp.bfloat16)
        for z in range(parts):
            out_ref[z, at, :] = out


def merge(got, c):
    parts, block, unused = got.shape
    block -= TAIL
    return pl.pallas_call(
        functools.partial(merge_kernel, c=c),
        out_shape=jax.ShapeDtypeStruct((parts, block, HEAD), jnp.bfloat16),
        compiler_params=pltpu.CompilerParams(vmem_limit_bytes=16 * MiB),
        name="merge",
    )(got)


def exchange(blocks, axis, order):
    return lax.all_to_all(
        blocks, axis, split_axis=0, concat_axis=0, axis_index_groups=[order], tiled=True
    )


def local(cache_keys, cache_values, counts, listed, queries):
    ctx_n = lax.axis_size("ctx")
    split_n = lax.axis_size("split")
    items, pages_here, page_len, head = cache_keys.shape
    requests = counts.shape[0]
    kv_heads = items // requests
    root = head**0.5
    c = head**-0.5
    item = lax.axis_index("ctx")
    split_idx = lax.axis_index("split")
    first = (item * split_n + split_idx) * pages_here
    message = pack(first.reshape(1), counts, listed, cache_keys, cache_values)
    got = exchange(message, "ctx", CTX)

    sel_row = lax.dynamic_index_in_dim(listed, item, 0, keepdims=False)
    count_row = lax.dynamic_index_in_dim(counts, item // kv_heads, 0, keepdims=False)
    mine = count_row.reshape(ctx_n, split_n, pages_here)
    mine = lax.dynamic_index_in_dim(mine, split_idx, 1, keepdims=False)
    mine = mine.reshape(4, 8, 2, pages_here).transpose(2, 0, 1, 3)
    mine = jnp.stack([mine[:, :, y] for y in RING], axis=2).reshape(ctx_n, pages_here)
    source = jnp.array(CTX, jnp.int32)[:, None]
    candidate = (source * split_n + split_idx) * pages_here + jnp.arange(
        pages_here, dtype=jnp.int32
    )
    marks = jnp.any(sel_row[None, None, :] == candidate[:, :, None], axis=2)
    live = jnp.sum(jnp.where(marks, mine, 0), axis=1)
    cbias = jnp.where(marks, NEG, jnp.log(mine.astype(jnp.float32)) * root)
    rows = queries.reshape(-1, head)
    partial = attend(live, cbias.reshape(1, -1), got, rows, split_n, c)
    shared = exchange(partial, "split", RING)
    out = exchange(merge(shared, c), "split", RING)
    out = jnp.concatenate([out[RING.index(z)] for z in range(split_n)], axis=0)
    return out.astype(jnp.float32).reshape(queries.shape)


def solution(mesh):
    return jax.shard_map(
        local,
        mesh=mesh,
        in_specs=(
            P(None, ("ctx", "split"), None, None),
            P(None, ("ctx", "split"), None, None),
            P(),
            P(),
            P("ctx", None, None, None),
        ),
        out_specs=P("ctx", None, None, None),
        check_vma=False,
    )
```

```python
import functools

import jax
import jax.numpy as jnp
from jax import lax
from jax.experimental import pallas as pl
from jax.experimental.pallas import tpu as pltpu
from jax.sharding import PartitionSpec as P

NEG = -1e30

PAGE = 64
HEAD = 128
TAIL = 8
ROWS = 2 * PAGE + TAIL
MiB = 1024 * 1024

RING = [3 * i % 8 for i in range(8)]
CTX = [(x * 8 + y) * 2 + core for core in range(2) for x in range(4) for y in RING]


GROUPS = [(0, 24), (24, 24), (48, 16)]
SENDS = [(at, 8) for at in range(0, 64, 8) if CTX[at] < 48]
SENDS += [(at, 1) for at in range(64) if CTX[at] >= 48]


def pack_kernel(
    page_ref,
    counts_ref,
    listed_ref,
    keys_ref,
    values_ref,
    out_ref,
    cache,
    message,
    count_here,
    listed,
    got,
    sent,
    small,
):
    items = out_ref.shape[0]
    page = page_ref[0]
    kv_heads = 4

    def fetch(g):
        at = pl.ds(GROUPS[g][0], GROUPS[g][1])
        return [
            pltpu.make_async_copy(ref.at[at], cache.at[a, at], got.at[a, g])
            for a, ref in enumerate((keys_ref, values_ref))
        ]

    def send(k):
        at = pl.ds(SENDS[k][0], SENDS[k][1])
        return pltpu.make_async_copy(message.at[at], out_ref.at[at], sent.at[k])

    columns = pl.ds(pl.multiple_of((page // HEAD) * HEAD, HEAD), HEAD)
    lists = pltpu.make_async_copy(listed_ref, listed, small.at[0])
    numbers = pltpu.make_async_copy(counts_ref.at[:, columns], count_here, small.at[1])
    lists.start()
    numbers.start()
    for g in range(len(GROUPS)):
        for a, copy in enumerate(fetch(g)):
            copy.start(priority=a)
    lists.wait()
    second = jnp.max(jnp.where(listed[...] == page + 1, 1.0, 0.0), axis=1, keepdims=True)
    numbers.wait()
    row = lax.broadcasted_iota(jnp.int32, (16, 4 * PAGE), 0)
    slot = lax.broadcasted_iota(jnp.int32, (16, 4 * PAGE), 1)
    quarter = slot // PAGE
    slot = slot % PAGE
    out_row = lax.broadcasted_iota(jnp.int32, (16, HEAD), 0)
    ready = set()
    for g, (first, number) in enumerate(GROUPS):
        for copy in fetch(g):
            copy.wait()
        for item in range(first, first + number):
            to = CTX.index(item)
            choice = jnp.broadcast_to(second[item : item + 1, :], (PAGE, HEAD)) > 0.5
            for a in range(2):
                message[to, a * PAGE : (a + 1) * PAGE, :] = jnp.where(
                    choice, cache[a, item, 1], cache[a, item, 0]
                )
        for item in range(first, first + number, 2):
            if item % kv_heads == 0:
                request = item // kv_heads
                count = [count_here[request, page % HEAD + p] for p in range(2)]
                limit = jnp.where(row % 2 == 0, count[0], count[1])
                live = jnp.logical_and(quarter == row, slot < limit)
                live = jnp.where(live, 1.0, 0.0).astype(jnp.bfloat16)
                divisor = jnp.where(out_row % 2 == 0, count[0], count[1]).astype(jnp.float32)
                inverse = 1.0 / divisor
            both = jnp.concatenate(
                [
                    jnp.concatenate([cache[a, i].reshape(2 * PAGE, HEAD) for a in range(2)], axis=0)
                    for i in (item, item + 1)
                ],
                axis=1,
            )
            total = jnp.dot(live, both, preferred_element_type=jnp.float32)
            for k in range(2):
                mean = total[:, k * HEAD : (k + 1) * HEAD] * inverse
                message[CTX.index(item + k), 2 * PAGE : ROWS, :] = mean[:TAIL].astype(jnp.bfloat16)
            ready.update((CTX.index(item), CTX.index(item + 1)))
            for k, (at, size) in enumerate(SENDS):
                if ready.issuperset(range(at, at + size)):
                    send(k).start(priority=k % 2)
                    ready.difference_update(range(at, at + size))
    for k in range(len(SENDS)):
        send(k).wait()


def pack(page, counts, listed, cache_keys, cache_values):
    items = cache_keys.shape[0]
    whole = pl.BlockSpec(memory_space=pl.ANY)
    return pl.pallas_call(
        pack_kernel,
        in_specs=[pl.BlockSpec(memory_space=pltpu.SMEM), whole, whole, whole, whole],
        out_specs=whole,
        out_shape=jax.ShapeDtypeStruct((items, ROWS, HEAD), jnp.bfloat16),
        scratch_shapes=[
            pltpu.VMEM((2, items, 2, PAGE, HEAD), jnp.bfloat16),
            pltpu.VMEM((items, ROWS, HEAD), jnp.bfloat16),
            pltpu.SMEM((counts.shape[0], HEAD), jnp.int32),
            pltpu.VMEM(listed.shape, jnp.int32),
            pltpu.SemaphoreType.DMA((2, len(GROUPS))),
            pltpu.SemaphoreType.DMA((len(SENDS),)),
            pltpu.SemaphoreType.DMA((2,)),
        ],
        compiler_params=pltpu.CompilerParams(vmem_limit_bytes=58 * MiB),
        name="pack",
    )(page, counts, listed, cache_keys, cache_values)


def split3(x):
    high = x.astype(jnp.bfloat16).astype(jnp.float32)
    rest = x - high
    middle = rest.astype(jnp.bfloat16).astype(jnp.float32)
    return high, middle, rest - middle


def attend_kernel(
    live_ref,
    cbias_ref,
    got_ref,
    q_ref,
    out_ref,
    keys,
    values,
    kt,
    vv,
    ckt,
    cv,
    cs,
    sc,
    best,
    top,
    acc,
    *,
    chunk,
    c,
):
    sources = got_ref.shape[0]
    cents = 2 * sources
    width = out_ref.shape[1] - TAIL
    block = sc.shape[0]

    tails = got_ref[:, 2 * PAGE : ROWS, :].astype(jnp.float32).reshape(sources * TAIL, HEAD)
    tails = tails.astype(jnp.bfloat16)
    r = lax.broadcasted_iota(jnp.int32, (cents, sources * TAIL), 0)
    col = lax.broadcasted_iota(jnp.int32, (cents, sources * TAIL), 1)
    first = (r // 2) * TAIL + r % 2
    cents_of = [
        jnp.dot(
            (col == first + off).astype(jnp.float32).astype(jnp.bfloat16),
            tails,
            preferred_element_type=jnp.float32,
        )
        for off in (0, 2)
    ]
    ckt[...] = jnp.transpose(cents_of[0]).astype(jnp.bfloat16)
    cv[:, :HEAD] = cents_of[1].astype(jnp.bfloat16)
    cv[:, HEAD:] = jnp.ones((cents, HEAD), jnp.bfloat16)

    def place(s, at):
        rows = pl.ds(at, PAGE)
        keys[rows, :] = got_ref[s, 0:PAGE, :].astype(jnp.float32)
        values[rows, :] = got_ref[s, PAGE : 2 * PAGE, :].astype(jnp.float32)
        return at + live_ref[s]

    end = lax.fori_loop(0, sources, place, 0, unroll=4)
    half = chunk // 2
    halves = (end + half - 1) // half
    large = 2 * chunk
    whole_chunks = halves // 4
    rest = pl.ds(end, chunk)
    keys[rest, :] = jnp.broadcast_to(keys[0:1, :], (chunk, HEAD))
    values[rest, :] = jnp.zeros((chunk, HEAD), jnp.float32)
    number = lax.broadcasted_iota(jnp.int32, (HEAD, HEAD), 0)

    def turn(j, carry):
        for k in range(0, chunk, HEAD):
            start = pl.multiple_of(j * chunk + k, HEAD)
            at = pl.ds(start, HEAD)
            kt[:, at] = jnp.transpose(keys[at, :]).astype(jnp.bfloat16)
            vv[at, :HEAD] = values[at, :].astype(jnp.bfloat16)
            vv[at, HEAD:] = jnp.where(number + start < end, 1.0, 0.0).astype(jnp.bfloat16)
        return carry

    lax.fori_loop(0, (halves + 1) // 2, turn, 0)

    def each_chunk(body):
        def whole(j, carry):
            body(pl.ds(pl.multiple_of(j * large, large), large))
            return carry

        lax.fori_loop(0, whole_chunks, whole, 0)
        left = halves % 4
        done = whole_chunks * large

        @pl.when(left >= 2)
        def _():
            body(pl.ds(pl.multiple_of(done, chunk), chunk))

        @pl.when(left % 2 == 1)
        def _():
            body(pl.ds(pl.multiple_of(done + (left // 2) * chunk, half), half))

    for first in range(0, q_ref.shape[0], block):
        score = jnp.dot(q_ref[first : first + block, :], ckt[...], preferred_element_type=jnp.float32) + cbias_ref[...]
        cs[...] = score
        best[...] = score

        def scores(at, first=first):
            score = jnp.dot(
                q_ref[first : first + block, :], kt[:, at], preferred_element_type=jnp.float32
            )
            sc[:, at] = score
            parts = [score[:, k : k + HEAD] for k in range(0, at.size, HEAD)]
            best[...] = jnp.maximum(best[...], functools.reduce(jnp.maximum, parts))

        each_chunk(scores)
        top[...] = jnp.broadcast_to(jnp.max(best[...], axis=1, keepdims=True), (block, HEAD))
        weight = jnp.exp((cs[...] - top[...]) * c).astype(jnp.bfloat16)
        acc[...] = jnp.dot(weight, cv[...], preferred_element_type=jnp.float32)

        def weighted(at):
            tops = jnp.concatenate([top[...]] * (at.size // HEAD), axis=1)
            weight = jnp.exp((sc[:, at] - tops) * c).astype(jnp.bfloat16)
            acc[...] += jnp.dot(weight, vv[at, :], preferred_element_type=jnp.float32)

        each_chunk(weighted)
        row = lax.broadcasted_iota(jnp.int32, (TAIL, HEAD), 0)
        for z in range(block // width):
            at = slice(z * width, (z + 1) * width)
            to = RING.index(first // width + z)
            total = acc[at, HEAD:]
            out_ref[to, :width, :] = (acc[at, :HEAD] / total).astype(jnp.bfloat16)
            stats = jnp.transpose(top[at, :] + jnp.log(total) * (1.0 / c))
            tile = jnp.zeros((TAIL, HEAD), jnp.float32)
            for i, piece in enumerate(split3(stats[0:1, :])):
                for h in range(2):
                    tile = jnp.where(row == 2 * i + h, piece[:, h * HEAD : (h + 1) * HEAD], tile)
            out_ref[to, width:, :] = tile.astype(jnp.bfloat16)


def attend(live, cbias, got, rows, parts, c):
    sources = got.shape[0]
    chunk = 512
    block = rows.shape[0] // 2
    slots = sources * PAGE
    cents = 2 * sources
    width = rows.shape[0] // parts
    vmem = pl.BlockSpec(memory_space=pltpu.VMEM)
    return pl.pallas_call(
        functools.partial(attend_kernel, chunk=chunk, c=c),
        in_specs=[pl.BlockSpec(memory_space=pltpu.SMEM), vmem, vmem, vmem],
        out_specs=vmem,
        scratch_shapes=[
            pltpu.VMEM((slots + chunk, HEAD), jnp.float32),
            pltpu.VMEM((slots + chunk, HEAD), jnp.float32),
            pltpu.VMEM((HEAD, slots), jnp.bfloat16),
            pltpu.VMEM((slots, 2 * HEAD), jnp.bfloat16),
            pltpu.VMEM((HEAD, cents), jnp.bfloat16),
            pltpu.VMEM((cents, 2 * HEAD), jnp.bfloat16),
            pltpu.VMEM((block, cents), jnp.float32),
            pltpu.VMEM((block, slots), jnp.float32),
            pltpu.VMEM((block, HEAD), jnp.float32),
            pltpu.VMEM((block, HEAD), jnp.float32),
            pltpu.VMEM((block, 2 * HEAD), jnp.float32),
        ],
        out_shape=jax.ShapeDtypeStruct((parts, width + TAIL, HEAD), jnp.bfloat16),
        compiler_params=pltpu.CompilerParams(vmem_limit_bytes=40 * MiB),
        cost_estimate=pl.CostEstimate(
            flops=4 * rows.shape[0] * (slots + cents) * HEAD,
            bytes_accessed=4 * MiB,
            transcendentals=rows.shape[0] * (slots + cents),
        ),
        name="attend",
    )(live, cbias, got, rows)


def merge_kernel(got_ref, out_ref, *, c):
    parts = got_ref.shape[0]
    block = out_ref.shape[1]
    sums = []
    for z in range(parts):
        tile = got_ref[z, block:, :].astype(jnp.float32)
        sums.append(tile[0:2] + tile[2:4] + tile[4:6])
    top = functools.reduce(jnp.maximum, sums)
    factors = [jnp.exp((m - top) * c) for m in sums]
    whole = functools.reduce(jnp.add, factors)
    columns = jnp.transpose(jnp.concatenate([f / whole for f in factors], axis=0))
    for h in range(2):
        at = slice(h * HEAD, (h + 1) * HEAD)
        out = jnp.zeros((HEAD, HEAD), jnp.float32)
        for z in range(parts):
            column = columns[:, 2 * z + h : 2 * z + h + 1]
            out += got_ref[z, at, :].astype(jnp.float32) * column
        out = out.astype(jnp.bfloat16)
        for z in range(parts):
            out_ref[z, at, :] = out


def merge(got, c):
    parts, block, unused = got.shape
    block -= TAIL
    return pl.pallas_call(
        functools.partial(merge_kernel, c=c),
        out_shape=jax.ShapeDtypeStruct((parts, block, HEAD), jnp.bfloat16),
        compiler_params=pltpu.CompilerParams(vmem_limit_bytes=16 * MiB),
        name="merge",
    )(got)


def exchange(blocks, axis, order):
    return lax.all_to_all(
        blocks, axis, split_axis=0, concat_axis=0, axis_index_groups=[order], tiled=True
    )


def local(cache_keys, cache_values, counts, listed, queries):
    ctx_n = lax.axis_size("ctx")
    split_n = lax.axis_size("split")
    items, pages_here, page_len, head = cache_keys.shape
    requests = counts.shape[0]
    kv_heads = items // requests
    root = head**0.5
    c = head**-0.5
    item = lax.axis_index("ctx")
    split_idx = lax.axis_index("split")
    first = (item * split_n + split_idx) * pages_here
    message = pack(first.reshape(1), counts, listed, cache_keys, cache_values)
    got = exchange(message, "ctx", CTX)

    sel_row = lax.dynamic_index_in_dim(listed, item, 0, keepdims=False)
    count_row = lax.dynamic_index_in_dim(counts, item // kv_heads, 0, keepdims=False)
    mine = count_row.reshape(ctx_n, split_n, pages_here)
    mine = lax.dynamic_index_in_dim(mine, split_idx, 1, keepdims=False)
    mine = mine.reshape(4, 8, 2, pages_here).transpose(2, 0, 1, 3)
    mine = jnp.stack([mine[:, :, y] for y in RING], axis=2).reshape(ctx_n, pages_here)
    source = jnp.array(CTX, jnp.int32)[:, None]
    candidate = (source * split_n + split_idx) * pages_here + jnp.arange(
        pages_here, dtype=jnp.int32
    )
    marks = jnp.any(sel_row[None, None, :] == candidate[:, :, None], axis=2)
    live = jnp.sum(jnp.where(marks, mine, 0), axis=1)
    cbias = jnp.where(marks, NEG, jnp.log(mine.astype(jnp.float32)) * root)
    rows = queries.reshape(-1, head)
    partial = attend(live, cbias.reshape(1, -1), got, rows, split_n, c)
    shared = exchange(partial, "split", RING)
    out = exchange(merge(shared, c), "split", RING)
    out = jnp.concatenate([out[RING.index(z)] for z in range(split_n)], axis=0)
    return out.astype(jnp.float32).reshape(queries.shape)


def solution(mesh):
    return jax.shard_map(
        local,
        mesh=mesh,
        in_specs=(
            P(None, ("ctx", "split"), None, None),
            P(None, ("ctx", "split"), None, None),
            P(),
            P(),
            P("ctx", None, None, None),
        ),
        out_specs=P("ctx", None, None, None),
        check_vma=False,
    )
```

```python
import functools

import jax
import jax.numpy as jnp
from jax import lax
from jax.experimental import pallas as pl
from jax.experimental.pallas import tpu as pltpu
from jax.sharding import PartitionSpec as P

NEG = -1e30

PAGE = 64
HEAD = 128
TAIL = 8
ROWS = 2 * PAGE + TAIL
MiB = 1024 * 1024

RING = [3 * i % 8 for i in range(8)]
CTX = [(x * 8 + y) * 2 + core for core in range(2) for x in range(4) for y in RING]


GROUPS = [(0, 24), (24, 24), (48, 16)]
SENDS = [(at, 8) for at in range(0, 64, 8) if CTX[at] < 48]
SENDS += [(at, 1) for at in range(64) if CTX[at] >= 48]


def pack_kernel(
    page_ref,
    counts_ref,
    listed_ref,
    keys_ref,
    values_ref,
    out_ref,
    cache,
    message,
    count_here,
    listed,
    got,
    sent,
    small,
):
    items = out_ref.shape[0]
    page = page_ref[0]
    kv_heads = 4

    def fetch(g):
        at = pl.ds(GROUPS[g][0], GROUPS[g][1])
        return [
            pltpu.make_async_copy(ref.at[at], cache.at[a, at], got.at[a, g])
            for a, ref in enumerate((keys_ref, values_ref))
        ]

    def send(k):
        at = pl.ds(SENDS[k][0], SENDS[k][1])
        return pltpu.make_async_copy(message.at[at], out_ref.at[at], sent.at[k])

    columns = pl.ds(pl.multiple_of((page // HEAD) * HEAD, HEAD), HEAD)
    lists = pltpu.make_async_copy(listed_ref, listed, small.at[0])
    numbers = pltpu.make_async_copy(counts_ref.at[:, columns], count_here, small.at[1])
    lists.start()
    numbers.start()
    for g in range(len(GROUPS)):
        for a, copy in enumerate(fetch(g)):
            copy.start(priority=a)
    lists.wait()
    second = jnp.max(jnp.where(listed[...] == page + 1, 1.0, 0.0), axis=1, keepdims=True)
    numbers.wait()
    row = lax.broadcasted_iota(jnp.int32, (16, 4 * PAGE), 0)
    slot = lax.broadcasted_iota(jnp.int32, (16, 4 * PAGE), 1)
    quarter = slot // PAGE
    slot = slot % PAGE
    out_row = lax.broadcasted_iota(jnp.int32, (16, HEAD), 0)
    ready = set()
    for g, (first, number) in enumerate(GROUPS):
        for copy in fetch(g):
            copy.wait()
        for item in range(first, first + number):
            to = CTX.index(item)
            choice = jnp.broadcast_to(second[item : item + 1, :], (PAGE, HEAD)) > 0.5
            for a in range(2):
                message[to, a * PAGE : (a + 1) * PAGE, :] = jnp.where(
                    choice, cache[a, item, 1], cache[a, item, 0]
                )
        for item in range(first, first + number, 2):
            if item % kv_heads == 0:
                request = item // kv_heads
                count = [count_here[request, page % HEAD + p] for p in range(2)]
                limit = jnp.where(row % 2 == 0, count[0], count[1])
                live = jnp.logical_and(quarter == row, slot < limit)
                live = jnp.where(live, 1.0, 0.0).astype(jnp.bfloat16)
                divisor = jnp.where(out_row % 2 == 0, count[0], count[1]).astype(jnp.float32)
                inverse = 1.0 / divisor
            both = jnp.concatenate(
                [
                    jnp.concatenate([cache[a, i].reshape(2 * PAGE, HEAD) for a in range(2)], axis=0)
                    for i in (item, item + 1)
                ],
                axis=1,
            )
            total = jnp.dot(live, both, preferred_element_type=jnp.float32)
            for k in range(2):
                mean = total[:, k * HEAD : (k + 1) * HEAD] * inverse
                message[CTX.index(item + k), 2 * PAGE : ROWS, :] = mean[:TAIL].astype(jnp.bfloat16)
            ready.update((CTX.index(item), CTX.index(item + 1)))
            for k, (at, size) in enumerate(SENDS):
                if ready.issuperset(range(at, at + size)):
                    send(k).start(priority=k % 2)
                    ready.difference_update(range(at, at + size))
    for k in range(len(SENDS)):
        send(k).wait()


def pack(page, counts, listed, cache_keys, cache_values):
    items = cache_keys.shape[0]
    whole = pl.BlockSpec(memory_space=pl.ANY)
    return pl.pallas_call(
        pack_kernel,
        in_specs=[pl.BlockSpec(memory_space=pltpu.SMEM), whole, whole, whole, whole],
        out_specs=whole,
        out_shape=jax.ShapeDtypeStruct((items, ROWS, HEAD), jnp.bfloat16),
        scratch_shapes=[
            pltpu.VMEM((2, items, 2, PAGE, HEAD), jnp.bfloat16),
            pltpu.VMEM((items, ROWS, HEAD), jnp.bfloat16),
            pltpu.SMEM((counts.shape[0], HEAD), jnp.int32),
            pltpu.VMEM(listed.shape, jnp.int32),
            pltpu.SemaphoreType.DMA((2, len(GROUPS))),
            pltpu.SemaphoreType.DMA((len(SENDS),)),
            pltpu.SemaphoreType.DMA((2,)),
        ],
        compiler_params=pltpu.CompilerParams(vmem_limit_bytes=58 * MiB),
        name="pack",
    )(page, counts, listed, cache_keys, cache_values)


def split3(x):
    high = x.astype(jnp.bfloat16).astype(jnp.float32)
    rest = x - high
    middle = rest.astype(jnp.bfloat16).astype(jnp.float32)
    return high, middle, rest - middle


def attend_kernel(
    live_ref,
    cbias_ref,
    got_ref,
    q_ref,
    out_ref,
    keys,
    values,
    kt,
    vv,
    ckt,
    cv,
    cs,
    sc,
    best,
    top,
    acc,
    *,
    chunk,
    c,
):
    sources = got_ref.shape[0]
    cents = 2 * sources
    width = out_ref.shape[1] - TAIL
    block = sc.shape[0]

    tails = got_ref[:, 2 * PAGE : ROWS, :].astype(jnp.float32).reshape(sources * TAIL, HEAD)
    tails = tails.astype(jnp.bfloat16)
    r = lax.broadcasted_iota(jnp.int32, (cents, sources * TAIL), 0)
    col = lax.broadcasted_iota(jnp.int32, (cents, sources * TAIL), 1)
    first = (r // 2) * TAIL + r % 2
    cents_of = [
        jnp.dot(
            (col == first + off).astype(jnp.float32).astype(jnp.bfloat16),
            tails,
            preferred_element_type=jnp.float32,
        )
        for off in (0, 2)
    ]
    ckt[...] = jnp.transpose(cents_of[0]).astype(jnp.bfloat16)
    cv[:, :HEAD] = cents_of[1].astype(jnp.bfloat16)
    cv[:, HEAD:] = jnp.ones((cents, HEAD), jnp.bfloat16)

    def place(s, at):
        rows = pl.ds(at, PAGE)
        keys[rows, :] = got_ref[s, 0:PAGE, :].astype(jnp.float32)
        values[rows, :] = got_ref[s, PAGE : 2 * PAGE, :].astype(jnp.float32)
        return at + live_ref[s]

    end = lax.fori_loop(0, sources, place, 0, unroll=4)
    half = chunk // 2
    halves = (end + half - 1) // half
    large = 4 * chunk
    whole_chunks = halves // 8
    rest = pl.ds(end, chunk)
    keys[rest, :] = jnp.broadcast_to(keys[0:1, :], (chunk, HEAD))
    values[rest, :] = jnp.zeros((chunk, HEAD), jnp.float32)
    number = lax.broadcasted_iota(jnp.int32, (HEAD, HEAD), 0)

    def turn(j, carry):
        for k in range(0, chunk, HEAD):
            start = pl.multiple_of(j * chunk + k, HEAD)
            at = pl.ds(start, HEAD)
            kt[:, at] = jnp.transpose(keys[at, :]).astype(jnp.bfloat16)
            vv[at, :HEAD] = values[at, :].astype(jnp.bfloat16)
            vv[at, HEAD:] = jnp.where(number + start < end, 1.0, 0.0).astype(jnp.bfloat16)
        return carry

    lax.fori_loop(0, (halves + 1) // 2, turn, 0)

    def each_chunk(body):
        def whole(j, carry):
            body(pl.ds(pl.multiple_of(j * large, large), large))
            return carry

        lax.fori_loop(0, whole_chunks, whole, 0)
        done = whole_chunks * 8
        for size in (4, 2, 1):
            need = (halves // size) % 2 == 1
            at = pl.ds(pl.multiple_of(done * half, half), size * half)
            pl.when(need)(functools.partial(body, at))
            done = done + jnp.where(need, size, 0)

    for first in range(0, q_ref.shape[0], block):
        score = jnp.dot(q_ref[first : first + block, :], ckt[...], preferred_element_type=jnp.float32) + cbias_ref[...]
        cs[...] = score
        best[...] = score

        def scores(at, first=first):
            score = jnp.dot(
                q_ref[first : first + block, :], kt[:, at], preferred_element_type=jnp.float32
            )
            sc[:, at] = score
            parts = [score[:, k : k + HEAD] for k in range(0, at.size, HEAD)]
            best[...] = jnp.maximum(best[...], functools.reduce(jnp.maximum, parts))

        each_chunk(scores)
        top[...] = jnp.broadcast_to(jnp.max(best[...], axis=1, keepdims=True), (block, HEAD))
        weight = jnp.exp((cs[...] - top[...]) * c).astype(jnp.bfloat16)
        acc[...] = jnp.dot(weight, cv[...], preferred_element_type=jnp.float32)

        def weighted(at):
            tops = jnp.concatenate([top[...]] * (at.size // HEAD), axis=1)
            weight = jnp.exp((sc[:, at] - tops) * c).astype(jnp.bfloat16)
            acc[...] += jnp.dot(weight, vv[at, :], preferred_element_type=jnp.float32)

        each_chunk(weighted)
        row = lax.broadcasted_iota(jnp.int32, (TAIL, HEAD), 0)
        for z in range(block // width):
            at = slice(z * width, (z + 1) * width)
            to = RING.index(first // width + z)
            total = acc[at, HEAD:]
            out_ref[to, :width, :] = (acc[at, :HEAD] / total).astype(jnp.bfloat16)
            stats = jnp.transpose(top[at, :] + jnp.log(total) * (1.0 / c))
            tile = jnp.zeros((TAIL, HEAD), jnp.float32)
            for i, piece in enumerate(split3(stats[0:1, :])):
                for h in range(2):
                    tile = jnp.where(row == 2 * i + h, piece[:, h * HEAD : (h + 1) * HEAD], tile)
            out_ref[to, width:, :] = tile.astype(jnp.bfloat16)


def attend(live, cbias, got, rows, parts, c):
    sources = got.shape[0]
    chunk = 512
    block = rows.shape[0] // 2
    slots = sources * PAGE
    cents = 2 * sources
    width = rows.shape[0] // parts
    vmem = pl.BlockSpec(memory_space=pltpu.VMEM)
    return pl.pallas_call(
        functools.partial(attend_kernel, chunk=chunk, c=c),
        in_specs=[pl.BlockSpec(memory_space=pltpu.SMEM), vmem, vmem, vmem],
        out_specs=vmem,
        scratch_shapes=[
            pltpu.VMEM((slots + chunk, HEAD), jnp.float32),
            pltpu.VMEM((slots + chunk, HEAD), jnp.float32),
            pltpu.VMEM((HEAD, slots), jnp.bfloat16),
            pltpu.VMEM((slots, 2 * HEAD), jnp.bfloat16),
            pltpu.VMEM((HEAD, cents), jnp.bfloat16),
            pltpu.VMEM((cents, 2 * HEAD), jnp.bfloat16),
            pltpu.VMEM((block, cents), jnp.float32),
            pltpu.VMEM((block, slots), jnp.float32),
            pltpu.VMEM((block, HEAD), jnp.float32),
            pltpu.VMEM((block, HEAD), jnp.float32),
            pltpu.VMEM((block, 2 * HEAD), jnp.float32),
        ],
        out_shape=jax.ShapeDtypeStruct((parts, width + TAIL, HEAD), jnp.bfloat16),
        compiler_params=pltpu.CompilerParams(vmem_limit_bytes=40 * MiB),
        cost_estimate=pl.CostEstimate(
            flops=4 * rows.shape[0] * (slots + cents) * HEAD,
            bytes_accessed=4 * MiB,
            transcendentals=rows.shape[0] * (slots + cents),
        ),
        name="attend",
    )(live, cbias, got, rows)


def merge_kernel(got_ref, out_ref, *, c):
    parts = got_ref.shape[0]
    block = out_ref.shape[1]
    sums = []
    for z in range(parts):
        tile = got_ref[z, block:, :].astype(jnp.float32)
        sums.append(tile[0:2] + tile[2:4] + tile[4:6])
    top = functools.reduce(jnp.maximum, sums)
    factors = [jnp.exp((m - top) * c) for m in sums]
    whole = functools.reduce(jnp.add, factors)
    columns = jnp.transpose(jnp.concatenate([f / whole for f in factors], axis=0))
    for h in range(2):
        at = slice(h * HEAD, (h + 1) * HEAD)
        out = jnp.zeros((HEAD, HEAD), jnp.float32)
        for z in range(parts):
            column = columns[:, 2 * z + h : 2 * z + h + 1]
            out += got_ref[z, at, :].astype(jnp.float32) * column
        out = out.astype(jnp.bfloat16)
        for z in range(parts):
            out_ref[z, at, :] = out


def merge(got, c):
    parts, block, unused = got.shape
    block -= TAIL
    return pl.pallas_call(
        functools.partial(merge_kernel, c=c),
        out_shape=jax.ShapeDtypeStruct((parts, block, HEAD), jnp.bfloat16),
        compiler_params=pltpu.CompilerParams(vmem_limit_bytes=16 * MiB),
        name="merge",
    )(got)


def exchange(blocks, axis, order):
    return lax.all_to_all(
        blocks, axis, split_axis=0, concat_axis=0, axis_index_groups=[order], tiled=True
    )


def local(cache_keys, cache_values, counts, listed, queries):
    ctx_n = lax.axis_size("ctx")
    split_n = lax.axis_size("split")
    items, pages_here, page_len, head = cache_keys.shape
    requests = counts.shape[0]
    kv_heads = items // requests
    root = head**0.5
    c = head**-0.5
    item = lax.axis_index("ctx")
    split_idx = lax.axis_index("split")
    first = (item * split_n + split_idx) * pages_here
    message = pack(first.reshape(1), counts, listed, cache_keys, cache_values)
    got = exchange(message, "ctx", CTX)

    sel_row = lax.dynamic_index_in_dim(listed, item, 0, keepdims=False)
    count_row = lax.dynamic_index_in_dim(counts, item // kv_heads, 0, keepdims=False)
    mine = count_row.reshape(ctx_n, split_n, pages_here)
    mine = lax.dynamic_index_in_dim(mine, split_idx, 1, keepdims=False)
    mine = mine.reshape(4, 8, 2, pages_here).transpose(2, 0, 1, 3)
    mine = jnp.stack([mine[:, :, y] for y in RING], axis=2).reshape(ctx_n, pages_here)
    source = jnp.array(CTX, jnp.int32)[:, None]
    candidate = (source * split_n + split_idx) * pages_here + jnp.arange(
        pages_here, dtype=jnp.int32
    )
    marks = jnp.any(sel_row[None, None, :] == candidate[:, :, None], axis=2)
    live = jnp.sum(jnp.where(marks, mine, 0), axis=1)
    cbias = jnp.where(marks, NEG, jnp.log(mine.astype(jnp.float32)) * root)
    rows = queries.reshape(-1, head)
    partial = attend(live, cbias.reshape(1, -1), got, rows, split_n, c)
    shared = exchange(partial, "split", RING)
    out = exchange(merge(shared, c), "split", RING)
    out = jnp.concatenate([out[RING.index(z)] for z in range(split_n)], axis=0)
    return out.astype(jnp.float32).reshape(queries.shape)


def solution(mesh):
    return jax.shard_map(
        local,
        mesh=mesh,
        in_specs=(
            P(None, ("ctx", "split"), None, None),
            P(None, ("ctx", "split"), None, None),
            P(),
            P(),
            P("ctx", None, None, None),
        ),
        out_specs=P("ctx", None, None, None),
        check_vma=False,
    )
```
